256 devices in a mesh: rows: 32 (over y, z), cols: 4 (over x_hi, core), views: 2 (over x_lo).
Axes of the slice: x: 4 (x_hi: 2, x_lo: 2; x = x_hi * 2 + x_lo), y: 4, z: 8, core: 2. Of those that a mesh axis runs over, the one named last changes fastest.
Arguments:
- queries: bfloat16 [2, 1024, 256, 384], P('views', 'rows', 'cols'), may hold values from -12 to 12
- key_rows: bfloat16 [2, 1024, 256, 384], P('views', 'rows', 'cols'), may hold values from -12 to 12
- value_rows: bfloat16 [2, 1024, 256, 384], P('views', 'rows', 'cols'), may hold values from -6 to 6
- grad_out: bfloat16 [2, 1024, 256, 384], P('views', 'rows', 'cols'), may hold values from -6 to 6
- regions: int32 [2, 1024, 256], P('views', 'rows', 'cols'), may hold values from 0 to 2
- flip_view: int32 [2], P('views'), may hold values from 0 to 7
- bias_table: float32 [12, 31, 31], replicated, may hold values from -4 to 4
- out_weight: bfloat16 [384, 384], replicated, may hold values from -0.3125 to 0.3125
Outputs:
- grad_queries: bfloat16 [2, 1024, 256, 384], P('views', 'rows', 'cols')
- grad_keys: bfloat16 [2, 1024, 256, 384], P('views', 'rows', 'cols')
- grad_values: bfloat16 [2, 1024, 256, 384], P('views', 'rows', 'cols')
- grad_weight: float32 [384, 384], replicated
The draws below stay inside these ranges and needn't reach their ends.
All inputs are finite; a program needn't handle non-finite values.
Results may differ from the reference program's by a relative error of at most 0.0058.
Values may be sent and summed in bfloat16 or wider, within the bound.
No kernel may reach another device: no remote copies, remote signals or barrier semaphores. Data moves between devices by JAX's collectives and lax.ppermute only.
A program may use at most 192 MiB of HBM per device.

```python
from functools import partial
import jax
import jax.numpy as jnp
from jax import lax

D = 384
HEADS = 12
WIN = 16
VIEWS = 2
BAND_H = 1024
BAND_W = 256


def draw_queries(key, part):
    key = jax.random.fold_in(key, 1)
    values_drawn = jax.random.normal(key, (VIEWS, BAND_H, BAND_W, D), jnp.float32)
    return jnp.clip(values_drawn, -12.0, 12.0).astype(jnp.bfloat16)


def draw_key_rows(key, part):
    key = jax.random.fold_in(key, 2)
    values_drawn = jax.random.normal(key, (VIEWS, BAND_H, BAND_W, D), jnp.float32)
    return jnp.clip(values_drawn, -12.0, 12.0).astype(jnp.bfloat16)


def with_ends(drawn, rng, low, largest):
    extent = drawn.shape
    place = [jax.random.randint(jax.random.fold_in(rng, axis), (), 0, extent[axis]) for axis in range(len(extent))]
    drawn = drawn.at[tuple(place)].set(low)
    longest = extent.index(max(extent))
    place[longest] = (place[longest] + 1) % extent[longest]
    return drawn.at[tuple(place)].set(largest)


def level_of(own_key, extent, cuts, smallest, high):
    def one(axis_at, parts):
        draws = jax.random.uniform(jax.random.fold_in(jax.random.fold_in(own_key, 6), axis_at), (parts,), jnp.float32, smallest / len(cuts), high / len(cuts))
        return jnp.repeat(jnp.exp(draws), extent[axis_at] // parts).reshape((-1,) + (1,) * (len(extent) - axis_at - 1))

    gain = one(*cuts[0])
    for cut in cuts[1:]:
        gain = gain * one(*cut)
    return gain


def centred(stream_key, shape, width, most, shards=(), held_as=jnp.bfloat16):
    drawn = jax.random.normal(stream_key, shape, jnp.float32) * width
    if len(shards) > 0:
        drawn = level_of(stream_key, shape, shards, -0.22, 0.18) * drawn
    return jnp.clip(drawn, min=-most, max=most).astype(held_as)


def setup_inputs(seed: int = 0) -> dict:
    arg_keys = jax.random.split(jax.random.key(seed), 9)
    return {
        "queries": draw_queries(jax.random.fold_in(arg_keys[8], 71), 0),
        "key_rows": draw_key_rows(jax.random.fold_in(arg_keys[8], 71), 0),
        "value_rows": centred(arg_keys[2], (VIEWS, BAND_H, BAND_W, D), 1.0, 6.0, ((0, 2), (1, 32), (2, 4))),
        "grad_out": centred(arg_keys[3], (VIEWS, BAND_H, BAND_W, D), 1.0, 6.0, ((0, 2), (1, 32), (2, 4))),
        "regions": with_ends(jax.random.randint(arg_keys[4], (VIEWS, BAND_H, BAND_W), 0, 3), jax.random.fold_in(arg_keys[4], 1), 0, 2).astype(jnp.int32),
        "flip_view": jax.random.randint(arg_keys[5], (VIEWS,), 0, 8).astype(jnp.int32),
        "bias_table": centred(arg_keys[6], (HEADS, 2 * WIN - 1, 2 * WIN - 1), 1.0, 4.0, (), jnp.float32),
        "out_weight": centred(arg_keys[7], (D, D), D ** -0.5, 0.3125),
    }


clip_norm = 384.0

def lowered(source):
    return lax.optimization_barrier(source.astype(jnp.bfloat16))

def split_heads(block):
    return block.astype(jnp.float32).reshape(block.shape[0], HEADS, -1)

def to_tiles(source):
    row_count, col_count = (source.shape[0], source.shape[1])
    shaped = source.reshape(row_count // WIN, WIN, col_count // WIN, WIN, source.shape[2])
    return shaped.transpose(0, 2, 1, 3, 4).reshape(-1, WIN * WIN, source.shape[2])

def from_tiles(tiles, row_count, col_count):
    shaped = tiles.reshape(row_count // WIN, col_count // WIN, WIN, WIN, tiles.shape[2])
    return shaped.transpose(0, 2, 1, 3, 4).reshape(row_count, col_count, tiles.shape[2])

def window_step(weight_sum, window_item, rel_bias, out_weight, scaling):
    blocks, key_code = window_item
    query_blk, key_blk, value_blk, grad_blk = blocks
    token_count = query_blk.shape[0]
    scores = jnp.einsum('phd,thd->hpt', split_heads(query_blk), split_heads(key_blk)) * scaling + rel_bias
    allowed = key_code[:, None] == key_code[None, :]
    scores = jnp.where(allowed[None], scores, -1e+30)
    row_peak = lax.optimization_barrier(jnp.max(scores, axis=-1, keepdims=True))
    expd_scores = jnp.exp(scores - row_peak)
    soft_probs = expd_scores / lax.optimization_barrier(jnp.sum(expd_scores, axis=-1, keepdims=True))
    probs_low = lowered(soft_probs)
    context = lowered(jnp.einsum('hpt,thd->phd', probs_low.astype(jnp.float32), split_heads(value_blk)).reshape(token_count, -1))
    weight_sum = weight_sum + jnp.dot(context.T, grad_blk, preferred_element_type=jnp.float32)
    grad_ctx = lowered(jnp.dot(grad_blk, out_weight.T, preferred_element_type=jnp.float32))
    grad_probs = jnp.einsum('phd,thd->hpt', split_heads(grad_ctx), split_heads(value_blk))
    grad_vals = jnp.einsum('hpt,phd->thd', probs_low.astype(jnp.float32), split_heads(grad_ctx))
    row_inner = lax.optimization_barrier(jnp.sum(soft_probs * grad_probs, axis=-1, keepdims=True))
    grad_scores = lowered(soft_probs * (grad_probs - row_inner) * scaling).astype(jnp.float32)
    grad_qry = jnp.einsum('hpt,thd->phd', grad_scores, split_heads(key_blk))
    grad_key = jnp.einsum('hpt,phd->thd', grad_scores, split_heads(query_blk))
    grad_tiles = tuple((result.reshape(token_count, -1).astype(jnp.bfloat16) for result in (grad_qry, grad_key, grad_vals)))
    return (weight_sum, grad_tiles)

def reference(queries, key_rows, value_rows, grad_out, regions, flip_view, bias_table, out_weight):
    half_win = WIN // 2
    scaling = (D // HEADS) ** (-0.5)
    offsets = jnp.arange(WIN * WIN, dtype=jnp.int32)
    pos_row = offsets // WIN
    pos_col = offsets % WIN
    row_side = ((jnp.arange(BAND_H, dtype=jnp.int32) + half_win) % BAND_H < half_win).astype(jnp.int32)
    col_side = ((jnp.arange(BAND_W, dtype=jnp.int32) + half_win) % BAND_W < half_win).astype(jnp.int32)
    weight_sum = jnp.zeros((D, D), jnp.float32)
    results = []
    for view_index in range(VIEWS):
        code = flip_view[view_index]
        col_sign = 1 - 2 * (code % 2)
        row_sign = 1 - 2 * (code // 2 % 2)
        row_idx = row_sign * (pos_row[None, :] - pos_row[:, None]) + WIN - 1
        col_idx = col_sign * (pos_col[None, :] - pos_col[:, None]) + WIN - 1
        rel_bias = jnp.where(code >= 4, bias_table[:, col_idx, row_idx], bias_table[:, row_idx, col_idx])
        key_code = regions[view_index] * 4 + row_side[:, None] * 2 + col_side[None, :]
        blocks = tuple((to_tiles(jnp.roll(source[view_index], (-half_win, -half_win), axis=(0, 1))) for source in (queries, key_rows, value_rows, grad_out)))
        window_codes = to_tiles(key_code[:, :, None])[:, :, 0]
        stepper = partial(window_step, rel_bias=rel_bias, out_weight=out_weight, scaling=scaling)
        weight_sum, grad_tiles = lax.scan(stepper, weight_sum, (blocks, window_codes))
        results.append(tuple((jnp.roll(from_tiles(grad_tile, BAND_H, BAND_W), (half_win, half_win), axis=(0, 1)) for grad_tile in grad_tiles)))
    norm_sq = jnp.sum(weight_sum * weight_sum)
    factor = jnp.minimum(1.0, clip_norm / jnp.sqrt(norm_sq + 1e-06))
    grad_weight = weight_sum * factor
    grad_queries = jnp.stack([entry[0] for entry in results])
    grad_keys = jnp.stack([entry[1] for entry in results])
    grad_values = jnp.stack([entry[2] for entry in results])
    return (grad_queries, grad_keys, grad_values, grad_weight)
```

```python
import math

import jax
import jax.numpy as jnp
from jax import lax
from jax.experimental import pallas as pl
from jax.experimental.pallas import tpu as pltpu
from jax.sharding import PartitionSpec as P

HEADS = 12
WIN = 16
HALF = 8
TOKENS = WIN * WIN
HEAD_DIM = 32
LANES = 128
PER_GROUP = LANES // HEAD_DIM
LOG2E = math.log2(math.e)
SCALING = HEAD_DIM**-0.5
FAR = 1e30
clip_norm = 384.0

f32 = jnp.float32
bf16 = jnp.bfloat16


def bias_kernel(table_ref, bias_ref):
    span = lax.broadcasted_iota(jnp.int32, (32, 512), 1)
    row_hot = (lax.broadcasted_iota(jnp.int32, (32, 512), 0) == 30 - span // WIN).astype(f32)
    wide = jnp.dot(
        table_ref[0], row_hot, preferred_element_type=f32, precision=lax.Precision.HIGHEST
    ) * LOG2E
    col_class = lax.broadcasted_iota(jnp.int32, (WIN, 512), 1) % WIN
    strip = jnp.zeros((WIN, 512), f32)
    for place in range(WIN):
        col = place ^ HALF
        piece = jnp.concatenate([wide[23 - col : 31 - col], wide[15 - col : 23 - col]], axis=0)
        strip = jnp.where(col_class == place, piece, strip)
    for place in range(WIN):
        start = WIN * (15 - (place ^ HALF))
        moved = pltpu.roll(strip, 512 - start, 1) if start else strip
        bias_ref[0, WIN * place : WIN * (place + 1)] = jnp.concatenate(
            [moved[:, LANES : 2 * LANES], moved[:, :LANES]], axis=1
        )


def build_bias(table, code):
    turned = jnp.where(code >= 4, jnp.swapaxes(table, 1, 2), table)
    turned = jnp.where((code // 2) % 2 == 1, turned[:, ::-1], turned)
    turned = jnp.where(code % 2 == 1, turned[:, :, ::-1], turned)
    turned = jnp.pad(jnp.swapaxes(turned, 1, 2), ((0, 0), (0, 1), (0, 1)))
    return pl.pallas_call(
        bias_kernel,
        grid=(HEADS,),
        in_specs=[pl.BlockSpec((1, 32, 32), lambda h: (h, 0, 0))],
        out_specs=pl.BlockSpec((1, TOKENS, TOKENS), lambda h: (h, 0, 0)),
        out_shape=jax.ShapeDtypeStruct((HEADS, TOKENS, TOKENS), f32),
        cost_estimate=pl.CostEstimate(flops=10**8, bytes_accessed=4 * 10**6, transcendentals=0),
        name="bias",
    )(turned)


def flipped(block):
    return block.astype(f32).T


def head_rows(block, j):
    parts = [block[HEAD_DIM * j : HEAD_DIM * (j + 1)]]
    if j > 0:
        parts.insert(0, jnp.zeros((HEAD_DIM * j, TOKENS), bf16))
    if j < PER_GROUP - 1:
        parts.append(jnp.zeros((LANES - HEAD_DIM * (j + 1), TOKENS), bf16))
    return jnp.concatenate(parts, axis=0)


def group_pass(q, k, v, g, code_row, weight, bias_ref):
    hot = (lax.broadcasted_iota(jnp.int32, (LANES, TOKENS), 0) == code_row).astype(f32)
    apart = (hot * -FAR).astype(bf16)
    keys_and_codes = jnp.concatenate([k, (1.0 - hot).T.astype(bf16)], axis=1)
    grad_ctx = lax.dot_general(g, weight, (((1,), (1,)), ((), ())), preferred_element_type=f32)
    grad_ctx_t = grad_ctx.T.astype(bf16)
    q_t, k_t, v_t = (flipped(block).astype(bf16) for block in (q, k, v))
    ones = jnp.ones((WIN, TOKENS), bf16)
    weights, scales, contexts, inners = [], [], [], []
    for j in range(PER_GROUP):
        own = slice(HEAD_DIM * j, HEAD_DIM * (j + 1))
        scores = jnp.dot(
            keys_and_codes,
            jnp.concatenate([head_rows(q_t, j), apart], axis=0),
            preferred_element_type=f32,
        )
        scores = scores * (LOG2E * SCALING) + bias_ref[j]
        peak = jnp.max(scores, axis=0, keepdims=True)
        expd = jnp.exp2(scores - peak).astype(bf16)
        summed = jnp.dot(
            jnp.concatenate([v_t[own], ones], axis=0), expd, preferred_element_type=f32
        )
        scale = 1.0 / summed[HEAD_DIM : HEAD_DIM + 1]
        context = summed[:HEAD_DIM] * scale
        inners.append(jnp.sum(context * grad_ctx_t[own].astype(f32), axis=0, keepdims=True))
        weights.append(expd)
        scales.append(scale)
        contexts.append(context.astype(bf16))
    weight_part = jnp.dot(jnp.concatenate(contexts, axis=0), g, preferred_element_type=f32)
    scale_cols = jnp.concatenate(
        [jnp.broadcast_to(scale, (HEAD_DIM, TOKENS)) for scale in scales], axis=0
    ).T
    q_scaled = (q.astype(f32) * (scale_cols * SCALING)).astype(bf16)
    grad_ctx_scaled = (grad_ctx * scale_cols).astype(bf16)
    lane_head = lax.broadcasted_iota(jnp.int32, (TOKENS, LANES), 1) // HEAD_DIM
    grad_q, grad_k, grad_v = [], None, None
    for j in range(PER_GROUP):
        own = slice(HEAD_DIM * j, HEAD_DIM * (j + 1))
        grad_probs = jnp.dot(v, head_rows(grad_ctx_t, j), preferred_element_type=f32)
        grad_scores = (weights[j].astype(f32) * (grad_probs - inners[j])).astype(bf16)
        grad_q.append(
            jnp.dot(k_t[own], grad_scores, preferred_element_type=f32) * (scales[j] * SCALING)
        )
        picked = lane_head == j
        for_k = jnp.where(picked, q_scaled, jnp.zeros_like(q_scaled))
        for_v = jnp.where(picked, grad_ctx_scaled, jnp.zeros_like(grad_ctx_scaled))
        more_k = jnp.dot(grad_scores, for_k, preferred_element_type=f32)
        more_v = jnp.dot(weights[j], for_v, preferred_element_type=f32)
        grad_k = more_k if grad_k is None else grad_k + more_k
        grad_v = more_v if grad_v is None else grad_v + more_v
    grad_q = jnp.concatenate(grad_q, axis=0).T
    return grad_q.astype(bf16), grad_k.astype(bf16), grad_v.astype(bf16), weight_part


def attend_kernel(q_ref, k_ref, v_ref, g_ref, code_ref, w_ref, bias_ref, gq_ref, gk_ref, gv_ref, ws_ref):
    window, group = pl.program_id(0), pl.program_id(1)
    rows = pl.ds(pl.multiple_of(group * LANES, LANES), LANES)
    grad_q, grad_k, grad_v, weight_part = group_pass(
        q_ref[0],
        k_ref[0],
        v_ref[0],
        g_ref[0],
        code_ref[0],
        w_ref[rows],
        bias_ref.at[pl.ds(group * PER_GROUP, PER_GROUP)],
    )
    gq_ref[0] = grad_q
    gk_ref[0] = grad_k
    gv_ref[0] = grad_v

    @pl.when(window == 0)
    def _():
        ws_ref[rows] = weight_part

    @pl.when(window > 0)
    def _():
        ws_ref[rows] += weight_part


def attend(blocks, codes, out_weight, bias, name):
    count, _, width = blocks[0].shape
    part = pl.BlockSpec((1, TOKENS, LANES), lambda w, g: (w, 0, g))
    whole = pl.BlockSpec((1, TOKENS, width), lambda w, g: (w, 0, 0))
    square = pl.BlockSpec((width, width), lambda w, g: (0, 0))
    grad = jax.ShapeDtypeStruct((count, TOKENS, width), bf16)
    return pl.pallas_call(
        attend_kernel,
        grid=(count, width // LANES),
        in_specs=[
            part,
            part,
            part,
            whole,
            pl.BlockSpec((1, 1, TOKENS), lambda w, g: (w, 0, 0)),
            square,
            pl.BlockSpec((HEADS, TOKENS, TOKENS), lambda w, g: (0, 0, 0)),
        ],
        out_specs=[part, part, part, square],
        out_shape=[grad, grad, grad, jax.ShapeDtypeStruct((width, width), f32)],
        compiler_params=pltpu.CompilerParams(vmem_limit_bytes=40 * 2**20),
        cost_estimate=pl.CostEstimate(
            flops=count * 10**9 * 3, bytes_accessed=count * 7 * 196608, transcendentals=0
        ),
        name=name,
    )(*blocks, codes, out_weight, bias)


def shifted(axis, distance):
    n = lax.axis_size(axis)
    return [(i, (i + distance) % n) for i in range(n)]


def shifted_both(row_distance, col_distance):
    rows, cols = lax.axis_size("rows"), lax.axis_size("cols")
    return [
        (r * cols + c, (r + row_distance) % rows * cols + (c + col_distance) % cols)
        for r in range(rows)
        for c in range(cols)
    ]


def natural(strip):
    rows, cols, width = strip.shape
    tiles = strip.reshape(rows, cols // WIN, WIN, width)
    low = lax.broadcasted_iota(jnp.int32, (1, 1, WIN, 1), 2) < HALF
    return jnp.where(low, tiles[:, 1:], tiles[:, :-1])


def xor_partners(axis, mask):
    n = 8 if axis == ("cols", "views") else lax.axis_size(axis)
    return [(i, i ^ mask) for i in range(n)]


def sum_over_all(part):
    place = lax.axis_index("cols") * 2 + lax.axis_index("views")
    near = ("cols", "views")
    masks = (2, 1, 4)
    flat = part.reshape(-1, LANES)
    bits = []
    for mask in masks:
        bit = (place // mask) % 2
        half = flat.shape[0] // 2
        keep = lax.dynamic_slice(flat, (bit * half, 0), (half, LANES))
        give = lax.dynamic_slice(flat, ((1 - bit) * half, 0), (half, LANES))
        flat = keep + lax.ppermute(give, near, xor_partners(near, mask))
        bits.append(bit)
    for mask in (1, 2, 4, 8, 16):
        flat = flat + lax.ppermute(flat, "rows", xor_partners("rows", mask))
    for mask, bit in zip(masks[::-1], bits[::-1]):
        other = lax.ppermute(flat, near, xor_partners(near, mask))
        flat = jnp.where(
            bit == 0, jnp.concatenate([flat, other]), jnp.concatenate([other, flat])
        )
    return flat.reshape(part.shape)


def body(queries, key_rows, value_rows, grad_out, regions, flip_view, bias_table, out_weight):
    arrays = [array[0] for array in (queries, key_rows, value_rows, grad_out)]
    width = arrays[0].shape[-1]
    tile_h, tile_w = arrays[0].shape[:2]
    band_h = tile_h * lax.axis_size("rows")
    band_w = tile_w * lax.axis_size("cols")
    up, down, left = shifted("rows", -1), shifted("rows", 1), shifted("cols", -1)

    from_below = lax.ppermute(
        jnp.stack([natural(a[:HALF])[:, :2] for a in arrays]), "rows", up
    )
    from_above = lax.ppermute(
        jnp.stack(
            [
                jnp.concatenate([natural(a[24:])[:, 2], a[24:, 56:]], axis=1)
                for a in arrays
            ]
        ),
        "rows",
        down,
    )
    from_right = lax.ppermute(jnp.stack([a[:24, :HALF] for a in arrays]), "cols", left)
    from_corner = lax.ppermute(
        jnp.stack([a[24:, :HALF] for a in arrays]), ("rows", "cols"), shifted_both(1, -1)
    )

    row_pos = (lax.axis_index("rows") * tile_h + jnp.arange(tile_h, dtype=jnp.int32) + HALF) % band_h
    col_pos = (lax.axis_index("cols") * tile_w + jnp.arange(tile_w, dtype=jnp.int32) + HALF) % band_w
    key_code = (
        regions[0] * 4
        + (row_pos < HALF).astype(jnp.int32)[:, None] * 2
        + (col_pos < HALF).astype(jnp.int32)[None, :]
    )
    codes = key_code.reshape(2, WIN, 4, WIN).transpose(0, 2, 1, 3)
    codes = jnp.roll(codes, (HALF, HALF), axis=(2, 3)).reshape(2, 4, 1, TOKENS)
    codes_above = lax.ppermute(codes[1, 2:], "rows", down)
    codes_late = jnp.concatenate([codes[1, :2], codes_above])

    bias = build_bias(bias_table, flip_view[0])

    early = []
    for a, beside in zip(arrays, from_right):
        inner = natural(a[HALF:24])
        border = jnp.concatenate([beside[HALF:], a[HALF:24, 56:]], axis=1)[:, None]
        rows = jnp.concatenate([inner, border], axis=1)
        rows = jnp.concatenate([rows[HALF:], rows[:HALF]], axis=0)
        early.append(rows.transpose(1, 0, 2, 3).reshape(4, TOKENS, width))
    late = []
    for a, below, above, beside, corner in zip(arrays, from_below, from_above, from_right, from_corner):
        lower = jnp.concatenate([below, natural(a[24:])[:, :2]], axis=0)
        upper = jnp.concatenate([natural(a[:HALF])[:, 2], above[:, :WIN]], axis=0)[:, None]
        edge = jnp.concatenate(
            [
                jnp.concatenate([beside[:HALF], a[:HALF, 56:]], axis=1),
                jnp.concatenate([corner, above[:, WIN:]], axis=1),
            ],
            axis=0,
        )[:, None]
        rows = jnp.concatenate([lower, upper, edge], axis=1)
        late.append(rows.transpose(1, 0, 2, 3).reshape(4, TOKENS, width))

    *early_grads, early_sum = attend(early, codes[0], out_weight, bias, "attend_early")
    *late_grads, late_sum = attend(late, codes_late, out_weight, bias, "attend_late")
    early_grads = [x.reshape(4, WIN, WIN, width) for x in early_grads]
    late_grads = [x.reshape(4, WIN, WIN, width) for x in late_grads]

    to_below = jnp.stack([x[:2, :HALF] for x in late_grads])
    to_above = jnp.stack(
        [jnp.concatenate([x[2, HALF:], x[3, HALF:, HALF:]], axis=1) for x in late_grads]
    )
    to_corner = jnp.stack([x[3, HALF:, :HALF] for x in late_grads])
    to_right = jnp.stack(
        [
            jnp.concatenate([x[3, :HALF, :HALF], y[3, :, :HALF]], axis=0)
            for x, y in zip(late_grads, early_grads)
        ]
    )
    home_below = lax.ppermute(to_below, "rows", down)
    home_above = lax.ppermute(to_above, "rows", up)
    home_corner = lax.ppermute(to_corner, ("rows", "cols"), shifted_both(-1, 1))
    home_right = lax.ppermute(to_right, "cols", shifted("cols", 1))

    weight_total = sum_over_all(early_sum + late_sum)

    grads = []
    for x, y, below, above, corner, beside in zip(
        late_grads, early_grads, home_below, home_above, home_corner, home_right
    ):
        top = [beside[:HALF]]
        for block in (below[0], below[1], x[2, :HALF]):
            top += [block[:, HALF:], block[:, :HALF]]
        top.append(x[3, :HALF, HALF:])
        middle = [jnp.concatenate([beside[WIN:], beside[HALF:WIN]], axis=0)]
        for w in range(3):
            block = jnp.concatenate([y[w, HALF:], y[w, :HALF]], axis=0)
            middle += [block[:, HALF:], block[:, :HALF]]
        middle.append(jnp.concatenate([y[3, HALF:, HALF:], y[3, :HALF, HALF:]], axis=0))
        bottom = [corner]
        for block in (x[0, HALF:], x[1, HALF:], above[:, :WIN]):
            bottom += [block[:, HALF:], block[:, :HALF]]
        bottom.append(above[:, WIN:])
        grads.append(
            jnp.concatenate([jnp.concatenate(part, axis=1) for part in (top, middle, bottom)], axis=0)
        )
    factor = jnp.minimum(1.0, clip_norm / jnp.sqrt(jnp.sum(weight_total * weight_total) + 1e-06))
    grad_weight = weight_total * factor
    return (grads[0][None], grads[1][None], grads[2][None], grad_weight)


def solution(mesh):
    return jax.shard_map(
        body,
        mesh=mesh,
        in_specs=(
            P("views", "rows", "cols", None),
            P("views", "rows", "cols", None),
            P("views", "rows", "cols", None),
            P("views", "rows", "cols", None),
            P("views", "rows", "cols"),
            P("views"),
            P(),
            P(),
        ),
        out_specs=(
            P("views", "rows", "cols", None),
            P("views", "rows", "cols", None),
            P("views", "rows", "cols", None),
            P(),
        ),
        check_vma=False,
    )
```

```python
import math

import jax
import jax.numpy as jnp
from jax import lax
from jax.experimental import pallas as pl
from jax.experimental.pallas import tpu as pltpu
from jax.sharding import PartitionSpec as P

HEADS = 12
WIN = 16
HALF = 8
TOKENS = WIN * WIN
HEAD_DIM = 32
LANES = 128
PER_GROUP = LANES // HEAD_DIM
PAIR = 2
VMEM = 60 * 2**20
LOG2E = math.log2(math.e)
SCALING = HEAD_DIM**-0.5
FAR = 1e30
clip_norm = 384.0

f32 = jnp.float32
bf16 = jnp.bfloat16


def bias_kernel(table_ref, bias_ref):
    span = lax.broadcasted_iota(jnp.int32, (32, 512), 1)
    row_hot = (lax.broadcasted_iota(jnp.int32, (32, 512), 0) == 30 - span // WIN).astype(f32)
    col_class = lax.broadcasted_iota(jnp.int32, (WIN, 512), 1) % WIN
    for head in range(PER_GROUP):
        wide = jnp.dot(
            table_ref[head], row_hot, preferred_element_type=f32, precision=lax.Precision.HIGHEST
        ) * LOG2E
        strip = jnp.zeros((WIN, 512), f32)
        for place in range(WIN):
            col = place ^ HALF
            piece = jnp.concatenate([wide[23 - col : 31 - col], wide[15 - col : 23 - col]], axis=0)
            strip = jnp.where(col_class == place, piece, strip)
        for place in range(WIN):
            start = WIN * (15 - (place ^ HALF))
            moved = pltpu.roll(strip, 512 - start, 1) if start else strip
            bias_ref[head, WIN * place : WIN * (place + 1)] = jnp.concatenate(
                [moved[:, LANES : 2 * LANES], moved[:, :LANES]], axis=1
            )


def build_bias(table, code):
    turned = jnp.where(code >= 4, jnp.swapaxes(table, 1, 2), table)
    turned = jnp.where((code // 2) % 2 == 1, turned[:, ::-1], turned)
    turned = jnp.where(code % 2 == 1, turned[:, :, ::-1], turned)
    turned = jnp.pad(jnp.swapaxes(turned, 1, 2), ((0, 0), (0, 1), (0, 1)))
    return pl.pallas_call(
        bias_kernel,
        grid=(HEADS // PER_GROUP,),
        in_specs=[pl.BlockSpec((PER_GROUP, 32, 32), lambda h: (h, 0, 0))],
        out_specs=pl.BlockSpec((PER_GROUP, TOKENS, TOKENS), lambda h: (h, 0, 0)),
        out_shape=jax.ShapeDtypeStruct((HEADS, TOKENS, TOKENS), f32),
        compiler_params=pltpu.CompilerParams(vmem_limit_bytes=VMEM),
        cost_estimate=pl.CostEstimate(flops=10**8, bytes_accessed=4 * 10**6, transcendentals=0),
        name="bias",
    )(turned)


def head_rows(block, j):
    parts = [block[HEAD_DIM * j : HEAD_DIM * (j + 1)]]
    if j > 0:
        parts.insert(0, jnp.zeros((HEAD_DIM * j, TOKENS), bf16))
    if j < PER_GROUP - 1:
        parts.append(jnp.zeros((LANES - HEAD_DIM * (j + 1), TOKENS), bf16))
    return jnp.concatenate(parts, axis=0)


def group_lanes(group):
    return slice(LANES * group, LANES * (group + 1))


def window_pass(cells, code_row, w_ref, bias_ref, store):
    g = cells(3, slice(None))
    hot = (lax.broadcasted_iota(jnp.int32, (LANES, TOKENS), 0) == code_row).astype(f32)
    apart = jnp.concatenate([(hot * -FAR).astype(bf16)] * PAIR, axis=1)
    codes_off = (1.0 - hot).astype(bf16).T
    grad_ctx = lax.dot_general(
        g, w_ref[...], (((1,), (1,)), ((), ())), preferred_element_type=f32
    )
    grad_ctx_t = grad_ctx.astype(bf16).T
    ones = jnp.ones((WIN, TOKENS), bf16)
    lane_head = lax.broadcasted_iota(jnp.int32, (TOKENS, LANES), 1) // HEAD_DIM
    groups, contexts = {}, []

    def open_group(n):
        q, k, v = (cells(i, group_lanes(n)) for i in range(3))
        groups[n] = dict(
            q=q, v=v, q_t=q.T, k_t=k.T, v_t=v.T,
            keys=jnp.concatenate([k, codes_off], axis=1),
            grad_ctx=grad_ctx[:, group_lanes(n)], grad_ctx_t=grad_ctx_t[group_lanes(n)],
            weights=[], scales=[], inners=[], grad_q=[], grad_scores=[],
        )

    def halves(both):
        return [both[:, TOKENS * i : TOKENS * (i + 1)] for i in range(PAIR)]

    def pair_rows(block, j):
        return jnp.concatenate([head_rows(block, j + i) for i in range(PAIR)], axis=1)

    def pair_scores(head):
        part = groups[head // PER_GROUP]
        right = jnp.concatenate([pair_rows(part["q_t"], head % PER_GROUP), apart], axis=0)
        return halves(jnp.dot(part["keys"], right, preferred_element_type=f32))

    def pair_grad_probs(head):
        part = groups[head // PER_GROUP]
        right = pair_rows(part["grad_ctx_t"], head % PER_GROUP)
        return halves(jnp.dot(part["v"], right, preferred_element_type=f32))

    def softmax(head, scores):
        part, j = groups[head // PER_GROUP], head % PER_GROUP
        own = slice(HEAD_DIM * j, HEAD_DIM * (j + 1))
        scores = scores * (LOG2E * SCALING) + bias_ref[head]
        expd = jnp.exp2(scores - jnp.max(scores, axis=0, keepdims=True)).astype(bf16)
        summed = jnp.dot(
            jnp.concatenate([part["v_t"][own], ones], axis=0), expd, preferred_element_type=f32
        )
        scale = 1.0 / summed[HEAD_DIM : HEAD_DIM + 1]
        context = summed[:HEAD_DIM] * scale
        part["inners"].append(
            jnp.sum(context * part["grad_ctx_t"][own].astype(f32), axis=0, keepdims=True)
        )
        part["weights"].append(expd)
        part["scales"].append(scale)
        contexts.append(context.astype(bf16))

    def score_grads(head, grad_probs):
        part, j = groups[head // PER_GROUP], head % PER_GROUP
        own = slice(HEAD_DIM * j, HEAD_DIM * (j + 1))
        grad_scores = (
            part["weights"][j].astype(f32) * (grad_probs - part["inners"][j])
        ).astype(bf16)
        part["grad_scores"].append(grad_scores)
        part["grad_q"].append(
            jnp.dot(part["k_t"][own], grad_scores, preferred_element_type=f32)
            * (part["scales"][j] * SCALING)
        )

    def stacked_heads(block):
        zero = jnp.zeros_like(block)
        return jnp.concatenate(
            [jnp.where(lane_head == j, block, zero) for j in range(PER_GROUP)], axis=0
        )

    def close_group(n):
        part = groups.pop(n)
        scale_cols = jnp.concatenate(
            [jnp.broadcast_to(scale, (HEAD_DIM, TOKENS)) for scale in part["scales"]], axis=0
        ).T
        q_scaled = (part["q"].astype(f32) * (scale_cols * SCALING)).astype(bf16)
        grad_ctx_scaled = (part["grad_ctx"] * scale_cols).astype(bf16)
        grad_k = jnp.dot(
            jnp.concatenate(part["grad_scores"], axis=1),
            stacked_heads(q_scaled),
            preferred_element_type=f32,
        )
        grad_v = jnp.dot(
            jnp.concatenate(part["weights"], axis=1),
            stacked_heads(grad_ctx_scaled),
            preferred_element_type=f32,
        )
        grad_q = jnp.concatenate(part["grad_q"], axis=0).astype(bf16).T
        store(group_lanes(n), grad_q, grad_k.astype(bf16), grad_v.astype(bf16))

    open_group(0)
    scores, grad_probs = {}, {}
    scores.update(zip(range(PAIR), pair_scores(0)))
    for first in range(0, HEADS + PAIR, PAIR):
        after = first + PAIR
        if after < HEADS:
            if after % PER_GROUP == 0:
                open_group(after // PER_GROUP)
            scores.update(zip(range(after, after + PAIR), pair_scores(after)))
        if first < HEADS:
            grad_probs.update(zip(range(first, after), pair_grad_probs(first)))
        for head in range(first, after):
            if head < HEADS:
                softmax(head, scores.pop(head))
            before = head - PAIR
            if before >= 0:
                score_grads(before, grad_probs.pop(before))
                if before % PER_GROUP == PER_GROUP - 1:
                    close_group(before // PER_GROUP)
    return jnp.dot(jnp.concatenate(contexts, axis=0), g, preferred_element_type=f32)


def merged(low, high):
    place = lax.broadcasted_iota(jnp.int32, low.shape, low.ndim - 2)
    return jnp.where(place < HALF, low, high)


def swapped(tiles):
    wide = tiles.astype(f32)
    return jnp.concatenate([wide[:, HALF:], wide[:, :HALF]], axis=1).astype(bf16)


def pack_low(tiles):
    n = tiles.shape[0] // 2
    return merged(tiles[:n], swapped(tiles[n:]))


def pack_high(tiles):
    n = tiles.shape[0] // 2
    return merged(swapped(tiles[n:]), tiles[:n])


def unpack(tiles):
    return jnp.concatenate([tiles, swapped(tiles)], axis=0)


def tile(ref, t, rows=slice(None)):
    return ref[rows, WIN * t : WIN * (t + 1), :]


def pack_kernel(*refs):
    ins, outs = refs[:12], refs[12:]
    up_ref, down_ref, corner_ref, left_ref = outs
    for i in range(4):
        top, bottom, middle = ins[3 * i : 3 * i + 3]
        for w in range(2):
            up_ref[i, w] = merged(tile(top, w + 1), tile(top, w))
        down_ref[i, :HALF] = merged(tile(bottom, 3), tile(bottom, 2))
        down_ref[i, HALF:] = pack_high(tile(bottom, 3))
        corner_ref[i] = pack_low(tile(bottom, 0))
        left_ref[i] = pack_low(middle[...])


def pack(arrays):
    width = arrays[0].shape[-1]
    top = pl.BlockSpec((HALF, 64, width), lambda i: (0, 0, 0))
    bottom = pl.BlockSpec((HALF, 64, width), lambda i: (3, 0, 0))
    middle = pl.BlockSpec((24, WIN, width), lambda i: (0, 0, 0))
    shapes = [(4, 2, HALF, WIN, width), (4, 12, WIN, width), (4, 4, WIN, width), (4, 12, WIN, width)]
    return pl.pallas_call(
        pack_kernel,
        grid=(1,),
        in_specs=[top, bottom, middle] * 4,
        out_specs=[pl.BlockSpec(s, lambda i, n=len(s): (0,) * n) for s in shapes],
        out_shape=[jax.ShapeDtypeStruct(s, bf16) for s in shapes],
        compiler_params=pltpu.CompilerParams(vmem_limit_bytes=VMEM),
        name="pack",
    )(*[a for a in arrays for _ in range(3)])


def early_kernel(*refs):
    tiles, (code_ref, w_ref, bias_ref, grad_ref, ws_ref, cells_ref) = refs[:16], refs[16:]

    @pl.when(pl.program_id(0) == 0)
    def _():
        ws_ref[...] = jnp.zeros_like(ws_ref)

    for i in range(4):
        upper, lower, upper_next, lower_next = (ref[...] for ref in tiles[4 * i : 4 * i + 4])
        cells_ref[i, :HALF] = merged(lower_next, lower)
        cells_ref[i, HALF:] = merged(upper_next, upper)

    def store(lanes, *grads):
        for i, grad in enumerate(grads):
            grad_ref[i, 0, :, :, lanes] = grad.reshape(WIN, WIN, LANES)

    ws_ref[...] += window_pass(
        lambda i, lanes: cells_ref[i, :, :, lanes].reshape(TOKENS, -1), code_ref[0], w_ref, bias_ref, store
    )


def attend_early(arrays, codes, out_weight, bias):
    width = arrays[0].shape[-1]
    corners = [
        pl.BlockSpec((HALF, WIN, width), lambda w, r=r, n=n: (r, w + n, 0))
        for n in (0, 1)
        for r in (1, 2)
    ]
    return pl.pallas_call(
        early_kernel,
        grid=(3,),
        in_specs=corners * 4
        + [
            pl.BlockSpec((1, 1, TOKENS), lambda w: (w, 0, 0)),
            pl.BlockSpec((width, width), lambda w: (0, 0)),
            pl.BlockSpec((HEADS, TOKENS, TOKENS), lambda w: (0, 0, 0)),
        ],
        out_specs=[
            pl.BlockSpec((3, 1, WIN, WIN, width), lambda w: (0, w, 0, 0, 0)),
            pl.BlockSpec((width, width), lambda w: (0, 0)),
        ],
        out_shape=[
            jax.ShapeDtypeStruct((3, 3, WIN, WIN, width), bf16),
            jax.ShapeDtypeStruct((width, width), f32),
        ],
        scratch_shapes=[pltpu.VMEM((4, WIN, WIN, width), bf16)],
        compiler_params=pltpu.CompilerParams(vmem_limit_bytes=VMEM),
        cost_estimate=pl.CostEstimate(flops=10**10, bytes_accessed=10**7, transcendentals=0),
        name="attend_early",
    )(*[a for a in arrays for _ in range(4)], codes, out_weight, bias)


def late_kernel(*refs):
    parts, refs = refs[:16], refs[16:]
    up_ref, down_ref, corner_ref, left_ref, code_ref, w_ref, bias_ref, before_ref = refs[:8]
    own_ref, below_ref, above_ref, corner_out_ref, right_ref, ws_ref, cells_ref = refs[8:]
    window = pl.program_id(0)

    @pl.when(window == 0)
    def _():
        ws_ref[...] = before_ref[...]
        for i in range(4):
            upper, lower = parts[4 * i + 2][...], parts[4 * i + 3][...]
            beside = unpack(left_ref[i])
            cells_ref[i, :HALF] = merged(beside[16:], lower)
            cells_ref[i, HALF:] = merged(beside[8:16], upper)

    for w in range(2):

        @pl.when(window == 1 + w)
        def _():
            for i in range(4):
                bottom = parts[4 * i + 1]
                cells_ref[i, :HALF] = up_ref[i, w]
                cells_ref[i, HALF:] = merged(tile(bottom, w + 1), tile(bottom, w))

    @pl.when(window == 3)
    def _():
        for i in range(4):
            top = parts[4 * i]
            cells_ref[i, :HALF] = merged(tile(top, 3), tile(top, 2))
            cells_ref[i, HALF:] = down_ref[i, :HALF]

    @pl.when(window == 4)
    def _():
        for i in range(4):
            top = parts[4 * i]
            cells_ref[i, :HALF] = merged(unpack(left_ref[i])[:HALF], tile(top, 3))
            cells_ref[i, HALF:] = merged(unpack(corner_ref[i]), unpack(down_ref[i, HALF:]))

    def store(lanes, *grads):
        for i, grad in enumerate(grads):
            own_ref[i, 0, :, :, lanes] = grad.reshape(WIN, WIN, LANES)

    ws_ref[...] += window_pass(
        lambda i, lanes: cells_ref[i, :, :, lanes].reshape(TOKENS, -1), code_ref[0], w_ref, bias_ref, store
    )

    @pl.when(window == 0)
    def _():
        for i in range(3):
            right_ref[i, 4:] = pack_low(own_ref[i, 0])

    for w in range(2):

        @pl.when(window == 1 + w)
        def _():
            for i in range(3):
                below_ref[i, w] = own_ref[i, 0, :HALF]

    @pl.when(window == 3)
    def _():
        for i in range(3):
            above_ref[i, :HALF] = own_ref[i, 0, HALF:]

    @pl.when(window == 4)
    def _():
        for i in range(3):
            above_ref[i, HALF:] = pack_high(own_ref[i, 0, HALF:])
            corner_out_ref[i] = pack_low(own_ref[i, 0, HALF:])
            right_ref[i, :4] = pack_low(own_ref[i, 0, :HALF])


def attend_late(arrays, borrowed, codes, out_weight, bias, before):
    width = arrays[0].shape[-1]
    fixed = lambda shape: pl.BlockSpec(shape, lambda w, n=len(shape): (0,) * n)
    parts = [
        pl.BlockSpec((HALF, 64, width), lambda w: (0, 0, 0)),
        pl.BlockSpec((HALF, 64, width), lambda w: (3, 0, 0)),
        pl.BlockSpec((HALF, WIN, width), lambda w: (1, 3, 0)),
        pl.BlockSpec((HALF, WIN, width), lambda w: (2, 3, 0)),
    ]
    back = [(3, 2, HALF, WIN, width), (3, 12, WIN, width), (3, 4, WIN, width), (3, 12, WIN, width)]
    return pl.pallas_call(
        late_kernel,
        grid=(5,),
        in_specs=parts * 4
        + [fixed(b.shape) for b in borrowed]
        + [
            pl.BlockSpec((1, 1, TOKENS), lambda w: (w, 0, 0)),
            fixed((width, width)),
            fixed((HEADS, TOKENS, TOKENS)),
            fixed((width, width)),
        ],
        out_specs=[pl.BlockSpec((3, 1, WIN, WIN, width), lambda w: (0, w, 0, 0, 0))]
        + [fixed(s) for s in back]
        + [fixed((width, width))],
        out_shape=[jax.ShapeDtypeStruct((3, 5, WIN, WIN, width), bf16)]
        + [jax.ShapeDtypeStruct(s, bf16) for s in back]
        + [jax.ShapeDtypeStruct((width, width), f32)],
        scratch_shapes=[pltpu.VMEM((4, WIN, WIN, width), bf16)],
        compiler_params=pltpu.CompilerParams(vmem_limit_bytes=VMEM),
        cost_estimate=pl.CostEstimate(flops=2 * 10**10, bytes_accessed=2 * 10**7, transcendentals=0),
        name="attend_late",
    )(*[a for a in arrays for _ in range(4)], *borrowed, codes, out_weight, bias, before)


def unpack_kernel(early_ref, late_ref, below_ref, above_ref, corner_ref, left_ref, *outs):
    for i, out in enumerate(outs):
        left, edge = unpack(left_ref[i, 4:]), unpack(left_ref[i, :4])
        above = unpack(above_ref[i, HALF:])

        def put(half, tiles):
            for t in range(4):
                rows = slice(HALF * half, HALF * (half + 1))
                out[rows, WIN * t : WIN * (t + 1), :] = merged(tiles[t], tiles[t + 1])

        put(0, [edge, below_ref[i, 0], below_ref[i, 1], late_ref[i, 3, :HALF], late_ref[i, 4, :HALF]])
        for half, rows in ((1, slice(HALF, WIN)), (2, slice(0, HALF))):
            own = [early_ref[i, w, rows] for w in range(3)] + [late_ref[i, 0, rows]]
            put(half, [left[rows]] + own)
        put(
            3,
            [unpack(corner_ref[i]), late_ref[i, 1, HALF:], late_ref[i, 2, HALF:], above_ref[i, :HALF], above],
        )


def unpack_all(pieces, width):
    fixed = lambda shape: pl.BlockSpec(shape, lambda i, n=len(shape): (0,) * n)
    out = (32, 64, width)
    return pl.pallas_call(
        unpack_kernel,
        grid=(1,),
        in_specs=[fixed(p.shape) for p in pieces],
        out_specs=[fixed(out)] * 3,
        out_shape=[jax.ShapeDtypeStruct(out, bf16)] * 3,
        compiler_params=pltpu.CompilerParams(vmem_limit_bytes=VMEM),
        name="unpack",
    )(*pieces)


def shifted(axis, distance):
    n = lax.axis_size(axis)
    return [(i, (i + distance) % n) for i in range(n)]


def shifted_both(row_distance, col_distance):
    rows, cols = lax.axis_size("rows"), lax.axis_size("cols")
    return [
        (r * cols + c, (r + row_distance) % rows * cols + (c + col_distance) % cols)
        for r in range(rows)
        for c in range(cols)
    ]


def xor_partners(axis, mask):
    n = 8 if axis == ("cols", "views") else lax.axis_size(axis)
    return [(i, i ^ mask) for i in range(n)]


def sum_over_all(part, between):
    place = lax.axis_index("cols") * 2 + lax.axis_index("views")
    near = ("cols", "views")
    masks = (2, 1, 4)
    share, bits = part, []
    for mask in masks:
        bit = (place // mask) % 2
        half = share.shape[0] // 2
        keep = lax.dynamic_slice_in_dim(share, bit * half, half)
        give = lax.dynamic_slice_in_dim(share, (1 - bit) * half, half)
        share = between(len(bits), keep + lax.ppermute(give, near, xor_partners(near, mask)))
        bits.append(bit)
    for step, mask in enumerate((1, 2, 4, 8, 16)):
        share = between(3 + step, share + lax.ppermute(share, "rows", xor_partners("rows", mask)))
    for step, (mask, bit) in enumerate(zip(masks[::-1], bits[::-1])):
        other = lax.ppermute(share, near, xor_partners(near, mask))
        share = between(
            8 + step,
            jnp.where(bit == 0, jnp.concatenate([share, other]), jnp.concatenate([other, share])),
        )
    return share


def body(queries, key_rows, value_rows, grad_out, regions, flip_view, bias_table, out_weight):
    arrays = [array[0] for array in (queries, key_rows, value_rows, grad_out)]
    width = arrays[0].shape[-1]
    tile_h, tile_w = arrays[0].shape[:2]
    band_h = tile_h * lax.axis_size("rows")
    band_w = tile_w * lax.axis_size("cols")
    up, down, left = shifted("rows", -1), shifted("rows", 1), shifted("cols", -1)

    to_up, to_down, to_corner, to_left = pack(arrays)
    borrowed = [
        lax.ppermute(to_up, "rows", up),
        lax.ppermute(to_down, "rows", down),
        lax.ppermute(to_corner, ("rows", "cols"), shifted_both(1, -1)),
        lax.ppermute(to_left, "cols", left),
    ]

    row_pos = (lax.axis_index("rows") * tile_h + jnp.arange(tile_h, dtype=jnp.int32) + HALF) % band_h
    col_pos = (lax.axis_index("cols") * tile_w + jnp.arange(tile_w, dtype=jnp.int32) + HALF) % band_w
    key_code = (
        regions[0] * 4
        + (row_pos < HALF).astype(jnp.int32)[:, None] * 2
        + (col_pos < HALF).astype(jnp.int32)[None, :]
    )
    codes = key_code.reshape(2, WIN, 4, WIN).transpose(0, 2, 1, 3)
    codes = jnp.roll(codes, (HALF, HALF), axis=(2, 3)).reshape(2, 4, 1, TOKENS)
    codes_above = lax.ppermute(codes[1, 2:], "rows", down)
    codes_late = jnp.concatenate([codes[0, 3:], codes[1, :2], codes_above])

    bias = build_bias(bias_table, flip_view[0])

    early, early_sum = attend_early(arrays, codes[0], out_weight, bias)
    late, to_below, to_above, to_corner, to_right, weight_part = attend_late(
        arrays, borrowed, codes_late, out_weight, bias, early_sum
    )

    home = [
        lax.ppermute(to_below, "rows", down),
        lax.ppermute(to_above, "rows", up),
        lax.ppermute(to_corner, ("rows", "cols"), shifted_both(-1, 1)),
        lax.ppermute(to_right, "cols", shifted("cols", 1)),
    ]
    grads = []

    def between(step, share):
        if step == 5:
            share, *home[:] = lax.optimization_barrier((share, *home))
        if step == 6:
            grads[:] = unpack_all([early, late, *home], width)
            share, *grads[:] = lax.optimization_barrier((share, *grads))
        return share

    weight_total = sum_over_all(weight_part, between)
    factor = jnp.minimum(1.0, clip_norm / jnp.sqrt(jnp.sum(weight_total * weight_total) + 1e-06))
    grad_weight = weight_total * factor
    return (grads[0][None], grads[1][None], grads[2][None], grad_weight)


def solution(mesh):
    return jax.shard_map(
        body,
        mesh=mesh,
        in_specs=(
            P("views", "rows", "cols", None),
            P("views", "rows", "cols", None),
            P("views", "rows", "cols", None),
            P("views", "rows", "cols", None),
            P("views", "rows", "cols"),
            P("views"),
            P(),
            P(),
        ),
        out_specs=(
            P("views", "rows", "cols", None),
            P("views", "rows", "cols", None),
            P("views", "rows", "cols", None),
            P(),
        ),
        check_vma=False,
    )
```

```python
import math
from functools import partial

import jax
import jax.numpy as jnp
from jax import lax
from jax.experimental import pallas as pl
from jax.experimental.pallas import tpu as pltpu
from jax.sharding import PartitionSpec as P

HEADS = 12
WIN = 16
HALF = 8
TOKENS = WIN * WIN
HEAD_DIM = 32
LANES = 128
PER_GROUP = LANES // HEAD_DIM
PAIR = 2
VMEM = 60 * 2**20
LOG2E = math.log2(math.e)
SCALING = HEAD_DIM**-0.5
FAR = 1e30
clip_norm = 384.0

f32 = jnp.float32
bf16 = jnp.bfloat16


def bias_kernel(table_ref, bias_ref):
    span = lax.broadcasted_iota(jnp.int32, (32, 512), 1)
    row_hot = (lax.broadcasted_iota(jnp.int32, (32, 512), 0) == 30 - span // WIN).astype(f32)
    col_class = lax.broadcasted_iota(jnp.int32, (WIN, 512), 1) % WIN
    for head in range(PER_GROUP):
        wide = jnp.dot(
            table_ref[head], row_hot, preferred_element_type=f32, precision=lax.Precision.HIGHEST
        ) * LOG2E
        strip = jnp.zeros((WIN, 512), f32)
        for place in range(WIN):
            col = place ^ HALF
            piece = jnp.concatenate([wide[23 - col : 31 - col], wide[15 - col : 23 - col]], axis=0)
            strip = jnp.where(col_class == place, piece, strip)
        for place in range(WIN):
            start = WIN * (15 - (place ^ HALF))
            moved = pltpu.roll(strip, 512 - start, 1) if start else strip
            bias_ref[head, WIN * place : WIN * (place + 1)] = jnp.concatenate(
                [moved[:, LANES : 2 * LANES], moved[:, :LANES]], axis=1
            )


def build_bias(table, code):
    turned = jnp.where(code >= 4, jnp.swapaxes(table, 1, 2), table)
    turned = jnp.where((code // 2) % 2 == 1, turned[:, ::-1], turned)
    turned = jnp.where(code % 2 == 1, turned[:, :, ::-1], turned)
    turned = jnp.pad(jnp.swapaxes(turned, 1, 2), ((0, 0), (0, 1), (0, 1)))
    return pl.pallas_call(
        bias_kernel,
        grid=(HEADS // PER_GROUP,),
        in_specs=[pl.BlockSpec((PER_GROUP, 32, 32), lambda h: (h, 0, 0))],
        out_specs=pl.BlockSpec((PER_GROUP, TOKENS, TOKENS), lambda h: (h, 0, 0)),
        out_shape=jax.ShapeDtypeStruct((HEADS, TOKENS, TOKENS), f32),
        compiler_params=pltpu.CompilerParams(vmem_limit_bytes=VMEM),
        cost_estimate=pl.CostEstimate(flops=10**8, bytes_accessed=4 * 10**6, transcendentals=0),
        name="bias",
    )(turned)


def head_rows(block, j):
    parts = [block[HEAD_DIM * j : HEAD_DIM * (j + 1)]]
    if j > 0:
        parts.insert(0, jnp.zeros((HEAD_DIM * j, TOKENS), bf16))
    if j < PER_GROUP - 1:
        parts.append(jnp.zeros((LANES - HEAD_DIM * (j + 1), TOKENS), bf16))
    return jnp.concatenate(parts, axis=0)


def group_lanes(group):
    return slice(LANES * group, LANES * (group + 1))


def projected(g, w_ref):
    grad_ctx = lax.dot_general(
        g, w_ref[...], (((1,), (1,)), ((), ())), preferred_element_type=f32
    )
    return grad_ctx, grad_ctx.astype(bf16).T


def halves(both):
    return [both[:, TOKENS * i : TOKENS * (i + 1)] for i in range(PAIR)]


def pair_rows(block, j):
    return jnp.concatenate([head_rows(block, j + i) for i in range(PAIR)], axis=1)


def own_rows(head):
    return slice(HEAD_DIM * (head % PER_GROUP), HEAD_DIM * (head % PER_GROUP + 1))


def forward_pass(cells, code_row, w_ref, bias_ref, keep_weights, stats_ref):
    g = cells(3, slice(None))
    hot = (lax.broadcasted_iota(jnp.int32, (LANES, TOKENS), 0) == code_row).astype(f32)
    apart = jnp.concatenate([(hot * -FAR).astype(bf16)] * PAIR, axis=1)
    codes_off = (1.0 - hot).astype(bf16).T
    _, grad_ctx_t = projected(g, w_ref)
    ones = jnp.ones((WIN, TOKENS), bf16)
    groups, contexts, scales, inners = {}, [], [], []

    def pair_scores(head):
        n = head // PER_GROUP
        if head % PER_GROUP == 0:
            q, k, v = (cells(i, group_lanes(n)) for i in range(3))
            groups[n] = q.T, v.T, jnp.concatenate([k, codes_off], axis=1)
        q_t, _, keys = groups[n]
        right = jnp.concatenate([pair_rows(q_t, head % PER_GROUP), apart], axis=0)
        return halves(jnp.dot(keys, right, preferred_element_type=f32))

    def softmax(head, scores):
        v_t = groups[head // PER_GROUP][1]
        scores = scores * (LOG2E * SCALING) + bias_ref[head]
        expd = jnp.exp2(scores - jnp.max(scores, axis=0, keepdims=True)).astype(bf16)
        keep_weights(head, expd)
        summed = jnp.dot(
            jnp.concatenate([v_t[own_rows(head)], ones], axis=0), expd, preferred_element_type=f32
        )
        scale = 1.0 / summed[HEAD_DIM : HEAD_DIM + 1]
        context = summed[:HEAD_DIM] * scale
        cotangent = grad_ctx_t[HEAD_DIM * head : HEAD_DIM * (head + 1)].astype(f32)
        inners.append(jnp.sum(context * cotangent, axis=0, keepdims=True))
        scales.append(scale)
        contexts.append(context.astype(bf16))

    scores = dict(zip(range(PAIR), pair_scores(0)))
    for first in range(0, HEADS, PAIR):
        after = first + PAIR
        if after < HEADS:
            scores.update(zip(range(after, after + PAIR), pair_scores(after)))
        for head in range(first, after):
            softmax(head, scores.pop(head))
    fill = jnp.zeros((WIN - HEADS, TOKENS), f32)
    stats_ref[0, 0] = jnp.concatenate(scales + [fill], axis=0)
    stats_ref[0, 1] = jnp.concatenate(inners + [fill], axis=0)
    return jnp.dot(jnp.concatenate(contexts, axis=0), g, preferred_element_type=f32)


def backward_pass(cells, weights, stats, w_ref, store):
    grad_ctx, grad_ctx_t = projected(cells(3, slice(None)), w_ref)
    lane_head = lax.broadcasted_iota(jnp.int32, (TOKENS, LANES), 1) // HEAD_DIM

    def stacked_heads(block):
        zero = jnp.zeros_like(block)
        return jnp.concatenate(
            [jnp.where(lane_head == j, block, zero) for j in range(PER_GROUP)], axis=0
        )

    def pair_grad_probs(head):
        n = head // PER_GROUP
        right = pair_rows(grad_ctx_t[group_lanes(n)], head % PER_GROUP)
        return halves(jnp.dot(cells(2, group_lanes(n)), right, preferred_element_type=f32))

    grad_probs = dict(zip(range(PAIR), pair_grad_probs(0)))
    for n in range(HEADS // PER_GROUP):
        q, k_t = cells(0, group_lanes(n)), cells(1, group_lanes(n)).T
        heads = range(PER_GROUP * n, PER_GROUP * (n + 1))
        grad_q, grad_scores = [], []
        for head in heads:
            after = head + PAIR
            if head % PAIR == 0 and after < HEADS:
                grad_probs.update(zip(range(after, after + PAIR), pair_grad_probs(after)))
            grad_scores.append(
                (weights(head).astype(f32) * (grad_probs.pop(head) - stats(1, head))).astype(bf16)
            )
            grad_q.append(
                jnp.dot(k_t[own_rows(head)], grad_scores[-1], preferred_element_type=f32)
                * (stats(0, head) * SCALING)
            )
        scale_cols = jnp.concatenate(
            [jnp.broadcast_to(stats(0, head), (HEAD_DIM, TOKENS)) for head in heads], axis=0
        ).T
        q_scaled = (q.astype(f32) * (scale_cols * SCALING)).astype(bf16)
        grad_ctx_scaled = (grad_ctx[:, group_lanes(n)] * scale_cols).astype(bf16)
        grad_k = jnp.dot(
            jnp.concatenate(grad_scores, axis=1), stacked_heads(q_scaled), preferred_element_type=f32
        )
        grad_v = jnp.dot(
            jnp.concatenate([weights(head) for head in heads], axis=1),
            stacked_heads(grad_ctx_scaled),
            preferred_element_type=f32,
        )
        grad_q = jnp.concatenate(grad_q, axis=0).astype(bf16).T
        store(group_lanes(n), grad_q, grad_k.astype(bf16), grad_v.astype(bf16))


def merged(low, high):
    place = lax.broadcasted_iota(jnp.int32, low.shape, low.ndim - 2)
    return jnp.where(place < HALF, low, high)


def swapped(tiles):
    wide = tiles.astype(f32)
    return jnp.concatenate([wide[:, HALF:], wide[:, :HALF]], axis=1).astype(bf16)


def pack_low(tiles):
    n = tiles.shape[0] // 2
    return merged(tiles[:n], swapped(tiles[n:]))


def pack_high(tiles):
    n = tiles.shape[0] // 2
    return merged(swapped(tiles[n:]), tiles[:n])


def unpack(tiles):
    return jnp.concatenate([tiles, swapped(tiles)], axis=0)


def tile(ref, t, rows=slice(None)):
    return ref[rows, WIN * t : WIN * (t + 1), :]


def pack_kernel(*refs):
    ins, outs = refs[:12], refs[12:]
    up_ref, down_ref, corner_ref, left_ref = outs
    for i in range(4):
        top, bottom, middle = ins[3 * i : 3 * i + 3]
        for w in range(2):
            up_ref[i, w] = merged(tile(top, w + 1), tile(top, w))
        down_ref[i, :HALF] = merged(tile(bottom, 3), tile(bottom, 2))
        down_ref[i, HALF:] = pack_high(tile(bottom, 3))
        corner_ref[i] = pack_low(tile(bottom, 0))
        left_ref[i] = pack_low(middle[...])


def pack(arrays):
    width = arrays[0].shape[-1]
    top = pl.BlockSpec((HALF, 64, width), lambda i: (0, 0, 0))
    bottom = pl.BlockSpec((HALF, 64, width), lambda i: (3, 0, 0))
    middle = pl.BlockSpec((24, WIN, width), lambda i: (0, 0, 0))
    shapes = [(4, 2, HALF, WIN, width), (4, 12, WIN, width), (4, 4, WIN, width), (4, 12, WIN, width)]
    return pl.pallas_call(
        pack_kernel,
        grid=(1,),
        in_specs=[top, bottom, middle] * 4,
        out_specs=[pl.BlockSpec(s, lambda i, n=len(s): (0,) * n) for s in shapes],
        out_shape=[jax.ShapeDtypeStruct(s, bf16) for s in shapes],
        compiler_params=pltpu.CompilerParams(vmem_limit_bytes=VMEM),
        name="pack",
    )(*[a for a in arrays for _ in range(3)])


def window_cells(cells_ref):
    return lambda i, lanes: cells_ref[i, 0, :, :, lanes].reshape(TOKENS, -1)


def run_forward(cells_ref, code_ref, w_ref, bias_ref, weights_ref, stats_ref):
    def keep_weights(head, expd):
        weights_ref[0, head] = expd

    return forward_pass(
        window_cells(cells_ref), code_ref[0], w_ref, bias_ref, keep_weights, stats_ref
    )


def early_kernel(*refs):
    tiles, (code_ref, w_ref, bias_ref, cells_ref, weights_ref, stats_ref, ws_ref) = refs[:16], refs[16:]

    @pl.when(pl.program_id(0) == 0)
    def _():
        ws_ref[...] = jnp.zeros_like(ws_ref)

    for i in range(4):
        upper, lower, upper_next, lower_next = (ref[...] for ref in tiles[4 * i : 4 * i + 4])
        cells_ref[i, 0, :HALF] = merged(lower_next, lower)
        cells_ref[i, 0, HALF:] = merged(upper_next, upper)
    ws_ref[...] += run_forward(cells_ref, code_ref, w_ref, bias_ref, weights_ref, stats_ref)


def fixed(shape):
    return pl.BlockSpec(shape, lambda w, n=len(shape): (0,) * n)


def forward_outs(count, width):
    specs = [
        pl.BlockSpec((4, 1, WIN, WIN, width), lambda w: (0, w, 0, 0, 0)),
        pl.BlockSpec((1, HEADS, TOKENS, TOKENS), lambda w: (w, 0, 0, 0)),
        pl.BlockSpec((1, 2, WIN, TOKENS), lambda w: (w, 0, 0, 0)),
        fixed((width, width)),
    ]
    shapes = [
        jax.ShapeDtypeStruct((4, count, WIN, WIN, width), bf16),
        jax.ShapeDtypeStruct((count, HEADS, TOKENS, TOKENS), bf16),
        jax.ShapeDtypeStruct((count, 2, WIN, TOKENS), f32),
        jax.ShapeDtypeStruct((width, width), f32),
    ]
    return specs, shapes


def forward_early(arrays, codes, out_weight, bias):
    width = arrays[0].shape[-1]
    corners = [
        pl.BlockSpec((HALF, WIN, width), lambda w, r=r, n=n: (r, w + n, 0))
        for n in (0, 1)
        for r in (1, 2)
    ]
    specs, shapes = forward_outs(3, width)
    return pl.pallas_call(
        early_kernel,
        grid=(3,),
        in_specs=corners * 4
        + [
            pl.BlockSpec((1, 1, TOKENS), lambda w: (w, 0, 0)),
            fixed((width, width)),
            fixed((HEADS, TOKENS, TOKENS)),
        ],
        out_specs=specs,
        out_shape=shapes,
        compiler_params=pltpu.CompilerParams(vmem_limit_bytes=VMEM),
        cost_estimate=pl.CostEstimate(flops=5 * 10**9, bytes_accessed=10**7, transcendentals=0),
        name="forward_early",
    )(*[a for a in arrays for _ in range(4)], codes, out_weight, bias)


def late_kernel(*refs):
    parts, refs = refs[:16], refs[16:]
    up_ref, down_ref, corner_ref, left_ref, code_ref, w_ref, bias_ref, before_ref = refs[:8]
    cells_ref, weights_ref, stats_ref, ws_ref = refs[8:]
    window = pl.program_id(0)

    for w in range(2):

        @pl.when(window == w)
        def _():
            for i in range(4):
                bottom = parts[4 * i + 1]
                cells_ref[i, 0, :HALF] = up_ref[i, w]
                cells_ref[i, 0, HALF:] = merged(tile(bottom, w + 1), tile(bottom, w))

    @pl.when(window == 2)
    def _():
        for i in range(4):
            top = parts[4 * i]
            cells_ref[i, 0, :HALF] = merged(tile(top, 3), tile(top, 2))
            cells_ref[i, 0, HALF:] = down_ref[i, :HALF]

    @pl.when(window == 3)
    def _():
        for i in range(4):
            top = parts[4 * i]
            cells_ref[i, 0, :HALF] = merged(unpack(left_ref[i])[:HALF], tile(top, 3))
            cells_ref[i, 0, HALF:] = merged(unpack(corner_ref[i]), unpack(down_ref[i, HALF:]))

    @pl.when(window == 4)
    def _():
        for i in range(4):
            upper, lower = parts[4 * i + 2][...], parts[4 * i + 3][...]
            beside = unpack(left_ref[i])
            cells_ref[i, 0, :HALF] = merged(beside[16:], lower)
            cells_ref[i, 0, HALF:] = merged(beside[8:16], upper)

    @pl.when(window == 0)
    def _():
        ws_ref[...] = before_ref[...]

    ws_ref[...] += run_forward(cells_ref, code_ref, w_ref, bias_ref, weights_ref, stats_ref)


def forward_late(arrays, borrowed, codes, out_weight, bias, before):
    width = arrays[0].shape[-1]
    parts = [
        pl.BlockSpec((HALF, 64, width), lambda w: (0, 0, 0)),
        pl.BlockSpec((HALF, 64, width), lambda w: (3, 0, 0)),
        pl.BlockSpec((HALF, WIN, width), lambda w: (1, 3, 0)),
        pl.BlockSpec((HALF, WIN, width), lambda w: (2, 3, 0)),
    ]
    specs, shapes = forward_outs(5, width)
    return pl.pallas_call(
        late_kernel,
        grid=(5,),
        in_specs=parts * 4
        + [fixed(b.shape) for b in borrowed]
        + [
            pl.BlockSpec((1, 1, TOKENS), lambda w: (w, 0, 0)),
            fixed((width, width)),
            fixed((HEADS, TOKENS, TOKENS)),
            fixed((width, width)),
        ],
        out_specs=specs,
        out_shape=shapes,
        compiler_params=pltpu.CompilerParams(vmem_limit_bytes=VMEM),
        cost_estimate=pl.CostEstimate(flops=10**10, bytes_accessed=2 * 10**7, transcendentals=0),
        name="forward_late",
    )(*[a for a in arrays for _ in range(4)], *borrowed, codes, out_weight, bias, before)


def backward(cells, weights, stats, out_weight, first, count, packs, name):
    width = cells.shape[-1]

    def kernel(cells_ref, weights_ref, stats_ref, w_ref, own_ref, *pack_refs):
        def store(lanes, *grads):
            for i, grad in enumerate(grads):
                own_ref[i, 0, :, :, lanes] = grad.reshape(WIN, WIN, LANES)

        backward_pass(
            window_cells(cells_ref),
            lambda head: weights_ref[0, head],
            lambda i, head: stats_ref[0, i, head : head + 1],
            w_ref,
            store,
        )
        for (_, writes), pack_ref in zip(packs, pack_refs):
            for window, write in writes:

                @pl.when(pl.program_id(0) == window - first)
                def _():
                    for i in range(3):
                        write(pack_ref, i, own_ref[i, 0])

    return pl.pallas_call(
        kernel,
        grid=(count,),
        in_specs=[
            pl.BlockSpec((4, 1, WIN, WIN, width), lambda w: (0, w + first, 0, 0, 0)),
            pl.BlockSpec((1, HEADS, TOKENS, TOKENS), lambda w: (w + first, 0, 0, 0)),
            pl.BlockSpec((1, 2, WIN, TOKENS), lambda w: (w + first, 0, 0, 0)),
            fixed((width, width)),
        ],
        out_specs=[pl.BlockSpec((3, 1, WIN, WIN, width), lambda w: (0, w, 0, 0, 0))]
        + [fixed(shape) for shape, _ in packs],
        out_shape=[jax.ShapeDtypeStruct((3, count, WIN, WIN, width), bf16)]
        + [jax.ShapeDtypeStruct(shape, bf16) for shape, _ in packs],
        compiler_params=pltpu.CompilerParams(vmem_limit_bytes=VMEM),
        cost_estimate=pl.CostEstimate(
            flops=count * 2 * 10**9, bytes_accessed=count * 3 * 10**6, transcendentals=0
        ),
        name=name,
    )(cells, weights, stats, out_weight)


def below_part(out, i, grads, window):
    out[i, window] = grads[:HALF]


def above_rows(out, i, grads):
    out[i, :HALF] = grads[HALF:]


def above_edge(out, i, grads):
    out[i, HALF:] = pack_high(grads[HALF:])


def corner_part(out, i, grads):
    out[i] = pack_low(grads[HALF:])


def right_edge(out, i, grads):
    out[i, :4] = pack_low(grads[:HALF])


def right_side(out, i, grads):
    out[i, 4:] = pack_low(grads)


def unpack_kernel(early_ref, lower_ref, upper_ref, below_ref, above_ref, corner_ref, left_ref, *outs):
    for i, out in enumerate(outs):
        left, edge = unpack(left_ref[i, 4:]), unpack(left_ref[i, :4])
        above = unpack(above_ref[i, HALF:])

        def put(half, tiles):
            for t in range(4):
                rows = slice(HALF * half, HALF * (half + 1))
                out[rows, WIN * t : WIN * (t + 1), :] = merged(tiles[t], tiles[t + 1])

        put(0, [edge, below_ref[i, 0], below_ref[i, 1], upper_ref[i, 0, :HALF], upper_ref[i, 1, :HALF]])
        for half, rows in ((1, slice(HALF, WIN)), (2, slice(0, HALF))):
            own = [early_ref[i, w, rows] for w in range(3)] + [upper_ref[i, 2, rows]]
            put(half, [left[rows]] + own)
        put(
            3,
            [unpack(corner_ref[i]), lower_ref[i, 0, HALF:], lower_ref[i, 1, HALF:], above_ref[i, :HALF], above],
        )


def unpack_all(pieces, width):
    out = (32, 64, width)
    return pl.pallas_call(
        unpack_kernel,
        grid=(1,),
        in_specs=[fixed(p.shape) for p in pieces],
        out_specs=[fixed(out)] * 3,
        out_shape=[jax.ShapeDtypeStruct(out, bf16)] * 3,
        compiler_params=pltpu.CompilerParams(vmem_limit_bytes=VMEM),
        name="unpack",
    )(*pieces)


def shifted(axis, distance):
    n = lax.axis_size(axis)
    return [(i, (i + distance) % n) for i in range(n)]


def shifted_both(row_distance, col_distance):
    rows, cols = lax.axis_size("rows"), lax.axis_size("cols")
    return [
        (r * cols + c, (r + row_distance) % rows * cols + (c + col_distance) % cols)
        for r in range(rows)
        for c in range(cols)
    ]


def xor_partners(axis, mask):
    n = 8 if axis == ("cols", "views") else lax.axis_size(axis)
    return [(i, i ^ mask) for i in range(n)]


def sum_over_all(part, between):
    place = lax.axis_index("cols") * 2 + lax.axis_index("views")
    near = ("cols", "views")
    masks = (2, 1, 5)
    labels = (place // 2 % 2, (place ^ place // 4) % 2, place // 4)
    share, bits = part, []
    for mask, bit in zip(masks, labels):
        half = share.shape[0] // 2
        keep = lax.dynamic_slice_in_dim(share, bit * half, half)
        give = lax.dynamic_slice_in_dim(share, (1 - bit) * half, half)
        share = between(len(bits), keep + lax.ppermute(give, near, xor_partners(near, mask)))
        bits.append(bit)
    for step, mask in enumerate((1, 3, 7, 8, 24)):
        share = between(3 + step, share + lax.ppermute(share, "rows", xor_partners("rows", mask)))
    for step, (mask, bit) in enumerate(zip(masks[::-1], bits[::-1])):
        other = lax.ppermute(share, near, xor_partners(near, mask))
        share = between(
            8 + step,
            jnp.where(bit == 0, jnp.concatenate([share, other]), jnp.concatenate([other, share])),
        )
    return share


def body(queries, key_rows, value_rows, grad_out, regions, flip_view, bias_table, out_weight):
    arrays = [array[0] for array in (queries, key_rows, value_rows, grad_out)]
    width = arrays[0].shape[-1]
    tile_h, tile_w = arrays[0].shape[:2]
    band_h = tile_h * lax.axis_size("rows")
    band_w = tile_w * lax.axis_size("cols")
    up, down, left = shifted("rows", -1), shifted("rows", 1), shifted("cols", -1)

    to_up, to_down, to_corner, to_left = pack(arrays)
    to_left, regions, flip_view = lax.optimization_barrier((to_left, regions, flip_view))
    borrowed = [
        lax.ppermute(to_up, "rows", up),
        lax.ppermute(to_down, "rows", down),
        lax.ppermute(to_corner, ("rows", "cols"), shifted_both(1, -1)),
        lax.ppermute(to_left, "cols", left),
    ]

    row_pos = (lax.axis_index("rows") * tile_h + jnp.arange(tile_h, dtype=jnp.int32) + HALF) % band_h
    col_pos = (lax.axis_index("cols") * tile_w + jnp.arange(tile_w, dtype=jnp.int32) + HALF) % band_w
    key_code = (
        regions[0] * 4
        + (row_pos < HALF).astype(jnp.int32)[:, None] * 2
        + (col_pos < HALF).astype(jnp.int32)[None, :]
    )
    codes = key_code.reshape(2, WIN, 4, WIN).transpose(0, 2, 1, 3)
    codes = jnp.roll(codes, (HALF, HALF), axis=(2, 3)).reshape(2, 4, 1, TOKENS)
    codes_above = lax.ppermute(codes[1, 2:], "rows", down)
    codes_late = jnp.concatenate([codes[1, :2], codes_above, codes[0, 3:]])

    bias = build_bias(bias_table, flip_view[0])

    cells_early, weights_early, stats_early, early_sum = forward_early(arrays, codes[0], out_weight, bias)
    cells_late, weights_late, stats_late, weight_part = forward_late(
        arrays, borrowed, codes_late, out_weight, bias, early_sum
    )

    held = {}

    def between(step, share):
        if step == 0:
            lower, to_below = backward(
                cells_late, weights_late, stats_late, out_weight, 0, 2,
                [((3, 2, HALF, WIN, width), [(w, partial(below_part, window=w)) for w in range(2)])],
                "backward_lower",
            )
            held["lower"] = lower
            share, to_below, held["late"] = lax.optimization_barrier((share, to_below, stats_late))
            held["below"] = lax.ppermute(to_below, "rows", down)
        if step == 1:
            held["upper"], to_above, to_corner, to_right = backward(
                cells_late, weights_late, held["late"], out_weight, 2, 3,
                [
                    ((3, 12, WIN, width), [(2, above_rows), (3, above_edge)]),
                    ((3, 4, WIN, width), [(3, corner_part)]),
                    ((3, 12, WIN, width), [(3, right_edge), (4, right_side)]),
                ],
                "backward_upper",
            )
            share, to_above, to_corner, to_right = lax.optimization_barrier(
                (share, to_above, to_corner, to_right)
            )
            held["home"] = [
                lax.ppermute(to_above, "rows", up),
                lax.ppermute(to_corner, ("rows", "cols"), shifted_both(-1, 1)),
                lax.ppermute(to_right, "cols", shifted("cols", 1)),
            ]
        if step == 2:
            share, held["early"] = lax.optimization_barrier((share, stats_early))
        if step == 3:
            held["inner"], = backward(
                cells_early, weights_early, held["early"], out_weight, 0, 3, [], "backward_early"
            )
            share, held["inner"] = lax.optimization_barrier((share, held["inner"]))
        if step == 6:
            share, *held["back"] = lax.optimization_barrier((share, held["below"], *held["home"]))
        if step == 7:
            grads = unpack_all([held["inner"], held["lower"], held["upper"], *held["back"]], width)
            share, *held["grads"] = lax.optimization_barrier((share, *grads))
        return share

    weight_total = sum_over_all(weight_part, between)
    grads = held["grads"]
    factor = jnp.minimum(1.0, clip_norm / jnp.sqrt(jnp.sum(weight_total * weight_total) + 1e-06))
    grad_weight = weight_total * factor
    return (grads[0][None], grads[1][None], grads[2][None], grad_weight)


def solution(mesh):
    return jax.shard_map(
        body,
        mesh=mesh,
        in_specs=(
            P("views", "rows", "cols", None),
            P("views", "rows", "cols", None),
            P("views", "rows", "cols", None),
            P("views", "rows", "cols", None),
            P("views", "rows", "cols"),
            P("views"),
            P(),
            P(),
        ),
        out_specs=(
            P("views", "rows", "cols", None),
            P("views", "rows", "cols", None),
            P("views", "rows", "cols", None),
            P(),
        ),
        check_vma=False,
    )
```

```python
import math

import jax
import jax.numpy as jnp
from jax import lax
from jax.experimental import pallas as pl
from jax.experimental.pallas import tpu as pltpu
from jax.sharding import PartitionSpec as P

HEADS = 12
WIN = 16
HALF = 8
TOKENS = WIN * WIN
HEAD_DIM = 32
LANES = 128
PER_GROUP = LANES // HEAD_DIM
PAIR = 2
VMEM = 60 * 2**20
LOG2E = math.log2(math.e)
SCALING = HEAD_DIM**-0.5
FAR = 1e30
clip_norm = 384.0

f32 = jnp.float32
bf16 = jnp.bfloat16


def bias_kernel(table_ref, bias_ref):
    span = lax.broadcasted_iota(jnp.int32, (32, 512), 1)
    row_hot = (lax.broadcasted_iota(jnp.int32, (32, 512), 0) == 30 - span // WIN).astype(f32)
    col_class = lax.broadcasted_iota(jnp.int32, (WIN, 512), 1) % WIN
    for head in range(PER_GROUP):
        wide = jnp.dot(
            table_ref[head], row_hot, preferred_element_type=f32, precision=lax.Precision.HIGHEST
        ) * LOG2E
        strip = jnp.zeros((WIN, 512), f32)
        for place in range(WIN):
            col = place ^ HALF
            piece = jnp.concatenate([wide[23 - col : 31 - col], wide[15 - col : 23 - col]], axis=0)
            strip = jnp.where(col_class == place, piece, strip)
        for place in range(WIN):
            start = WIN * (15 - (place ^ HALF))
            moved = pltpu.roll(strip, 512 - start, 1) if start else strip
            bias_ref[head, WIN * place : WIN * (place + 1)] = jnp.concatenate(
                [moved[:, LANES : 2 * LANES], moved[:, :LANES]], axis=1
            )


def build_bias(table, code):
    turned = jnp.where(code >= 4, jnp.swapaxes(table, 1, 2), table)
    turned = jnp.where((code // 2) % 2 == 1, turned[:, ::-1], turned)
    turned = jnp.where(code % 2 == 1, turned[:, :, ::-1], turned)
    turned = jnp.pad(jnp.swapaxes(turned, 1, 2), ((0, 0), (0, 1), (0, 1)))
    return pl.pallas_call(
        bias_kernel,
        grid=(HEADS // PER_GROUP,),
        in_specs=[pl.BlockSpec((PER_GROUP, 32, 32), lambda h: (h, 0, 0))],
        out_specs=pl.BlockSpec((PER_GROUP, TOKENS, TOKENS), lambda h: (h, 0, 0)),
        out_shape=jax.ShapeDtypeStruct((HEADS, TOKENS, TOKENS), f32),
        compiler_params=pltpu.CompilerParams(vmem_limit_bytes=VMEM),
        cost_estimate=pl.CostEstimate(flops=10**8, bytes_accessed=4 * 10**6, transcendentals=0),
        name="bias",
    )(turned)


def head_rows(block, j):
    parts = [block[HEAD_DIM * j : HEAD_DIM * (j + 1)]]
    if j > 0:
        parts.insert(0, jnp.zeros((HEAD_DIM * j, TOKENS), bf16))
    if j < PER_GROUP - 1:
        parts.append(jnp.zeros((LANES - HEAD_DIM * (j + 1), TOKENS), bf16))
    return jnp.concatenate(parts, axis=0)


def group_lanes(group):
    return slice(LANES * group, LANES * (group + 1))


def window_pass(cells, code_row, w_ref, bias_refs, store):
    g = cells(3, slice(None))
    hot = (lax.broadcasted_iota(jnp.int32, (LANES, TOKENS), 0) == code_row).astype(f32)
    apart = jnp.concatenate([(hot * -FAR).astype(bf16)] * PAIR, axis=1)
    codes_off = (1.0 - hot).astype(bf16).T
    grad_ctx = lax.dot_general(
        g, w_ref[...], (((1,), (1,)), ((), ())), preferred_element_type=f32
    )
    grad_ctx_t = grad_ctx.astype(bf16).T
    ones = jnp.ones((WIN, TOKENS), bf16)
    lane_head = lax.broadcasted_iota(jnp.int32, (TOKENS, LANES), 1) // HEAD_DIM
    groups, contexts = {}, []

    def open_group(n):
        q, k, v = (cells(i, group_lanes(n)) for i in range(3))
        groups[n] = dict(
            q=q, v=v, q_t=q.T, k_t=k.T, v_t=v.T,
            keys=jnp.concatenate([k, codes_off], axis=1),
            grad_ctx=grad_ctx[:, group_lanes(n)], grad_ctx_t=grad_ctx_t[group_lanes(n)],
            weights=[], scales=[], inners=[], grad_q=[], grad_scores=[],
        )

    def halves(both):
        return [both[:, TOKENS * i : TOKENS * (i + 1)] for i in range(PAIR)]

    def pair_rows(block, j):
        return jnp.concatenate([head_rows(block, j + i) for i in range(PAIR)], axis=1)

    def pair_scores(head):
        part = groups[head // PER_GROUP]
        right = jnp.concatenate([pair_rows(part["q_t"], head % PER_GROUP), apart], axis=0)
        return halves(jnp.dot(part["keys"], right, preferred_element_type=f32))

    def pair_grad_probs(head):
        part = groups[head // PER_GROUP]
        right = pair_rows(part["grad_ctx_t"], head % PER_GROUP)
        return halves(jnp.dot(part["v"], right, preferred_element_type=f32))

    def softmax(head, scores):
        part, j = groups[head // PER_GROUP], head % PER_GROUP
        own = slice(HEAD_DIM * j, HEAD_DIM * (j + 1))
        scores = scores * (LOG2E * SCALING) + bias_refs[head // PER_GROUP][j]
        expd = jnp.exp2(scores - jnp.max(scores, axis=0, keepdims=True)).astype(bf16)
        summed = jnp.dot(
            jnp.concatenate([part["v_t"][own], ones], axis=0), expd, preferred_element_type=f32
        )
        scale = 1.0 / summed[HEAD_DIM : HEAD_DIM + 1]
        context = summed[:HEAD_DIM] * scale
        part["inners"].append(
            jnp.sum(context * part["grad_ctx_t"][own].astype(f32), axis=0, keepdims=True)
        )
        part["weights"].append(expd)
        part["scales"].append(scale)
        contexts.append(context.astype(bf16))

    def score_grads(head, grad_probs):
        part, j = groups[head // PER_GROUP], head % PER_GROUP
        own = slice(HEAD_DIM * j, HEAD_DIM * (j + 1))
        grad_scores = (
            part["weights"][j].astype(f32) * (grad_probs - part["inners"][j])
        ).astype(bf16)
        part["grad_scores"].append(grad_scores)
        part["grad_q"].append(
            jnp.dot(part["k_t"][own], grad_scores, preferred_element_type=f32)
            * (part["scales"][j] * SCALING)
        )

    def stacked_heads(block):
        zero = jnp.zeros_like(block)
        return jnp.concatenate(
            [jnp.where(lane_head == j, block, zero) for j in range(PER_GROUP)], axis=0
        )

    def close_group(n):
        part = groups.pop(n)
        scale_cols = jnp.concatenate(
            [jnp.broadcast_to(scale, (HEAD_DIM, TOKENS)) for scale in part["scales"]], axis=0
        ).T
        q_scaled = (part["q"].astype(f32) * (scale_cols * SCALING)).astype(bf16)
        grad_ctx_scaled = (part["grad_ctx"] * scale_cols).astype(bf16)
        grad_k = jnp.dot(
            jnp.concatenate(part["grad_scores"], axis=1),
            stacked_heads(q_scaled),
            preferred_element_type=f32,
        )
        grad_v = jnp.dot(
            jnp.concatenate(part["weights"], axis=1),
            stacked_heads(grad_ctx_scaled),
            preferred_element_type=f32,
        )
        grad_q = jnp.concatenate(part["grad_q"], axis=0).astype(bf16).T
        store(group_lanes(n), grad_q, grad_k.astype(bf16), grad_v.astype(bf16))

    open_group(0)
    scores, grad_probs = {}, {}
    scores.update(zip(range(PAIR), pair_scores(0)))
    for first in range(0, HEADS + PAIR, PAIR):
        after = first + PAIR
        if after < HEADS:
            if after % PER_GROUP == 0:
                open_group(after // PER_GROUP)
            scores.update(zip(range(after, after + PAIR), pair_scores(after)))
        if first < HEADS:
            grad_probs.update(zip(range(first, after), pair_grad_probs(first)))
        for head in range(first, after):
            if head < HEADS:
                softmax(head, scores.pop(head))
            before = head - PAIR
            if before >= 0:
                score_grads(before, grad_probs.pop(before))
                if before % PER_GROUP == PER_GROUP - 1:
                    close_group(before // PER_GROUP)
    return jnp.dot(jnp.concatenate(contexts, axis=0), g, preferred_element_type=f32)


def merged(low, high):
    place = lax.broadcasted_iota(jnp.int32, low.shape, low.ndim - 2)
    return jnp.where(place < HALF, low, high)


def swapped(tiles):
    wide = tiles.astype(f32)
    return jnp.concatenate([wide[:, HALF:], wide[:, :HALF]], axis=1).astype(bf16)


def pack_low(tiles):
    n = tiles.shape[0] // 2
    return merged(tiles[:n], swapped(tiles[n:]))


def pack_high(tiles):
    n = tiles.shape[0] // 2
    return merged(swapped(tiles[n:]), tiles[:n])


def unpack(tiles):
    return jnp.concatenate([tiles, swapped(tiles)], axis=0)


def tile(ref, t, rows=slice(None)):
    return ref[rows, WIN * t : WIN * (t + 1), :]


def pack_kernel(*refs):
    ins, outs = refs[:12], refs[12:]
    up_ref, down_ref, corner_ref, left_ref = outs
    for i in range(4):
        top, bottom, middle = ins[3 * i : 3 * i + 3]
        for w in range(2):
            up_ref[i, w] = merged(tile(top, w + 1), tile(top, w))
        down_ref[i, :HALF] = merged(tile(bottom, 3), tile(bottom, 2))
        down_ref[i, HALF:] = pack_high(tile(bottom, 3))
        corner_ref[i] = pack_low(tile(bottom, 0))
        left_ref[i] = pack_low(middle[...])


def pack(arrays):
    width = arrays[0].shape[-1]
    top = pl.BlockSpec((HALF, 64, width), lambda i: (0, 0, 0))
    bottom = pl.BlockSpec((HALF, 64, width), lambda i: (3, 0, 0))
    middle = pl.BlockSpec((24, WIN, width), lambda i: (0, 0, 0))
    shapes = [(4, 2, HALF, WIN, width), (4, 12, WIN, width), (4, 4, WIN, width), (4, 12, WIN, width)]
    return pl.pallas_call(
        pack_kernel,
        grid=(1,),
        in_specs=[top, bottom, middle] * 4,
        out_specs=[pl.BlockSpec(s, lambda i, n=len(s): (0,) * n) for s in shapes],
        out_shape=[jax.ShapeDtypeStruct(s, bf16) for s in shapes],
        compiler_params=pltpu.CompilerParams(vmem_limit_bytes=VMEM),
        name="pack",
    )(*[a for a in arrays for _ in range(3)])


def bias_specs():
    return [
        pl.BlockSpec((PER_GROUP, TOKENS, TOKENS), lambda w, n=n: (n, 0, 0))
        for n in range(HEADS // PER_GROUP)
    ]


def early_kernel(*refs):
    tiles, (code_ref, w_ref), bias_refs = refs[:16], refs[16:18], refs[18:21]
    grad_ref, ws_ref, cells_ref = refs[21:]

    @pl.when(pl.program_id(0) == 0)
    def _():
        ws_ref[...] = jnp.zeros_like(ws_ref)

    for i in range(4):
        upper, lower, upper_next, lower_next = (ref[...] for ref in tiles[4 * i : 4 * i + 4])
        cells_ref[i, :HALF] = merged(lower_next, lower)
        cells_ref[i, HALF:] = merged(upper_next, upper)

    def store(lanes, *grads):
        for i, grad in enumerate(grads):
            grad_ref[i, 0, :, :, lanes] = grad.reshape(WIN, WIN, LANES)

    ws_ref[...] += window_pass(
        lambda i, lanes: cells_ref[i, :, :, lanes].reshape(TOKENS, -1), code_ref[0, 0], w_ref, bias_refs, store
    )


def attend_early(arrays, codes, out_weight, bias):
    width = arrays[0].shape[-1]
    corners = [
        pl.BlockSpec((HALF, WIN, width), lambda w, r=r, n=n: (r, w + n, 0))
        for n in (0, 1)
        for r in (1, 2)
    ]
    return pl.pallas_call(
        early_kernel,
        grid=(3,),
        in_specs=corners * 4
        + [
            pl.BlockSpec((1, 1, 1, TOKENS), lambda w: (0, w, 0, 0)),
            pl.BlockSpec((width, width), lambda w: (0, 0)),
        ]
        + bias_specs(),
        out_specs=[
            pl.BlockSpec((3, 1, WIN, WIN, width), lambda w: (0, w, 0, 0, 0)),
            pl.BlockSpec((width, width), lambda w: (0, 0)),
        ],
        out_shape=[
            jax.ShapeDtypeStruct((3, 3, WIN, WIN, width), bf16),
            jax.ShapeDtypeStruct((width, width), f32),
        ],
        scratch_shapes=[pltpu.VMEM((4, WIN, WIN, width), bf16)],
        compiler_params=pltpu.CompilerParams(vmem_limit_bytes=VMEM),
        cost_estimate=pl.CostEstimate(flops=10**10, bytes_accessed=10**7, transcendentals=0),
        name="attend_early",
    )(*[a for a in arrays for _ in range(4)], codes, out_weight, bias, bias, bias)


def late_kernel(*refs):
    parts, refs = refs[:8], refs[8:]
    up_ref, down_ref, corner_ref, left_ref, code_ref, code_above_ref, w_ref, before_ref = refs[:8]
    bias_refs, refs = refs[8:11], refs[11:]
    own_ref, below_ref, above_ref, corner_out_ref, right_ref, ws_ref, cells_ref = refs
    window = pl.program_id(0)

    @pl.when(window == 0)
    def _():
        ws_ref[...] = before_ref[...]

    @pl.when(window < 2)
    def _():
        for i in range(4):
            cells_ref[i, :HALF] = up_ref[i, 0]
            cells_ref[i, HALF:] = merged(parts[2 * i + 1][...], parts[2 * i][...])

    @pl.when(window == 2)
    def _():
        for i in range(4):
            cells_ref[i, :HALF] = merged(parts[2 * i + 1][...], parts[2 * i][...])
            cells_ref[i, HALF:] = down_ref[i, :HALF]

    @pl.when(window == 3)
    def _():
        for i in range(4):
            cells_ref[i, :HALF] = merged(unpack(left_ref[i])[:HALF], parts[2 * i][...])
            cells_ref[i, HALF:] = merged(unpack(corner_ref[i]), unpack(down_ref[i, HALF:]))

    @pl.when(window == 4)
    def _():
        for i in range(4):
            beside = unpack(left_ref[i])
            cells_ref[i, :HALF] = merged(beside[16:], parts[2 * i + 1][...])
            cells_ref[i, HALF:] = merged(beside[8:16], parts[2 * i][...])

    above = (window == 2) | (window == 3)
    code_row = jnp.where(above, code_above_ref[0], code_ref[0, 0])

    def store(lanes, *grads):
        for i, grad in enumerate(grads):
            own_ref[i, 0, :, :, lanes] = grad.reshape(WIN, WIN, LANES)

    ws_ref[...] += window_pass(
        lambda i, lanes: cells_ref[i, :, :, lanes].reshape(TOKENS, -1), code_row, w_ref, bias_refs, store
    )

    for w in range(2):

        @pl.when(window == w)
        def _():
            for i in range(3):
                below_ref[i, w] = own_ref[i, 0, :HALF]

    @pl.when(window == 2)
    def _():
        for i in range(3):
            above_ref[i, :HALF] = own_ref[i, 0, HALF:]

    @pl.when(window == 4)
    def _():
        for i in range(3):
            right_ref[i, 4:] = pack_low(own_ref[i, 0])

    @pl.when(window == 3)
    def _():
        for i in range(3):
            above_ref[i, HALF:] = pack_high(own_ref[i, 0, HALF:])
            corner_out_ref[i] = pack_low(own_ref[i, 0, HALF:])
            right_ref[i, :4] = pack_low(own_ref[i, 0, :HALF])


def attend_late(arrays, borrowed, codes, codes_above, out_weight, bias, before):
    width = arrays[0].shape[-1]
    fixed = lambda shape: pl.BlockSpec(shape, lambda w, n=len(shape): (0,) * n)

    def rows_of(w, side):
        return jnp.where(w < 2, 3, jnp.where(w < 4, 0, 1 + side))

    parts = [
        pl.BlockSpec((HALF, WIN, width), lambda w: (rows_of(w, 0), jnp.minimum(w, 3), 0)),
        pl.BlockSpec((HALF, WIN, width), lambda w: (rows_of(w, 1), jnp.minimum(w + 1, 3), 0)),
    ]
    up_spec = pl.BlockSpec((4, 1, HALF, WIN, width), lambda w: (0, jnp.minimum(w, 1), 0, 0, 0))
    back = [(3, 2, HALF, WIN, width), (3, 12, WIN, width), (3, 4, WIN, width), (3, 12, WIN, width)]
    return pl.pallas_call(
        late_kernel,
        grid=(5,),
        in_specs=parts * 4
        + [up_spec]
        + [fixed(b.shape) for b in borrowed[1:]]
        + [
            pl.BlockSpec(
                (1, 1, 1, TOKENS),
                lambda w: (jnp.where(w < 4, 1, 0), jnp.where(w < 2, w, 3), 0, 0),
            ),
            pl.BlockSpec((1, 1, TOKENS), lambda w: (jnp.where(w == 3, 1, 0), 0, 0)),
            fixed((width, width)),
            fixed((width, width)),
        ]
        + bias_specs(),
        out_specs=[pl.BlockSpec((3, 1, WIN, WIN, width), lambda w: (0, w, 0, 0, 0))]
        + [fixed(s) for s in back]
        + [fixed((width, width))],
        out_shape=[jax.ShapeDtypeStruct((3, 5, WIN, WIN, width), bf16)]
        + [jax.ShapeDtypeStruct(s, bf16) for s in back]
        + [jax.ShapeDtypeStruct((width, width), f32)],
        scratch_shapes=[pltpu.VMEM((4, WIN, WIN, width), bf16)],
        compiler_params=pltpu.CompilerParams(vmem_limit_bytes=VMEM),
        cost_estimate=pl.CostEstimate(flops=2 * 10**10, bytes_accessed=2 * 10**7, transcendentals=0),
        name="attend_late",
    )(
        *[a for a in arrays for _ in range(2)],
        *borrowed,
        codes,
        codes_above,
        out_weight,
        before,
        bias,
        bias,
        bias,
    )


def unpack_kernel(early_ref, late_ref, below_ref, above_ref, corner_ref, left_ref, *outs):
    for i, out in enumerate(outs):
        left, edge = unpack(left_ref[i, 4:]), unpack(left_ref[i, :4])
        above = unpack(above_ref[i, HALF:])

        def put(half, tiles):
            for t in range(4):
                rows = slice(HALF * half, HALF * (half + 1))
                out[rows, WIN * t : WIN * (t + 1), :] = merged(tiles[t], tiles[t + 1])

        put(0, [edge, below_ref[i, 0], below_ref[i, 1], late_ref[i, 2, :HALF], late_ref[i, 3, :HALF]])
        for half, rows in ((1, slice(HALF, WIN)), (2, slice(0, HALF))):
            own = [early_ref[i, w, rows] for w in range(3)] + [late_ref[i, 4, rows]]
            put(half, [left[rows]] + own)
        put(
            3,
            [unpack(corner_ref[i]), late_ref[i, 0, HALF:], late_ref[i, 1, HALF:], above_ref[i, :HALF], above],
        )


def unpack_all(pieces, width):
    fixed = lambda shape: pl.BlockSpec(shape, lambda i, n=len(shape): (0,) * n)
    out = (32, 64, width)
    return pl.pallas_call(
        unpack_kernel,
        grid=(1,),
        in_specs=[fixed(p.shape) for p in pieces],
        out_specs=[fixed(out)] * 3,
        out_shape=[jax.ShapeDtypeStruct(out, bf16)] * 3,
        compiler_params=pltpu.CompilerParams(vmem_limit_bytes=VMEM),
        name="unpack",
    )(*pieces)


def shifted(axis, distance):
    n = lax.axis_size(axis)
    return [(i, (i + distance) % n) for i in range(n)]


def shifted_both(row_distance, col_distance):
    rows, cols = lax.axis_size("rows"), lax.axis_size("cols")
    return [
        (r * cols + c, (r + row_distance) % rows * cols + (c + col_distance) % cols)
        for r in range(rows)
        for c in range(cols)
    ]


def xor_partners(axis, mask):
    n = 8 if axis == ("cols", "views") else lax.axis_size(axis)
    return [(i, i ^ mask) for i in range(n)]


def sum_over_all(part, between):
    place = lax.axis_index("cols") * 2 + lax.axis_index("views")
    near = ("cols", "views")
    masks = (2, 1, 5)
    labels = (place // 2 % 2, (place ^ place // 4) % 2, place // 4)
    share, bits = part, []
    for mask, bit in zip(masks, labels):
        half = share.shape[0] // 2
        keep = lax.dynamic_slice_in_dim(share, bit * half, half)
        give = lax.dynamic_slice_in_dim(share, (1 - bit) * half, half)
        share = between(len(bits), keep + lax.ppermute(give, near, xor_partners(near, mask)))
        bits.append(bit)
    for step, mask in enumerate((1, 3, 7, 8, 24)):
        share = between(3 + step, share + lax.ppermute(share, "rows", xor_partners("rows", mask)))
    for step, (mask, bit) in enumerate(zip(masks[::-1], bits[::-1])):
        other = lax.ppermute(share, near, xor_partners(near, mask))
        share = between(
            8 + step,
            jnp.where(bit == 0, jnp.concatenate([share, other]), jnp.concatenate([other, share])),
        )
    return share


def body(queries, key_rows, value_rows, grad_out, regions, flip_view, bias_table, out_weight):
    arrays = [array[0] for array in (queries, key_rows, value_rows, grad_out)]
    width = arrays[0].shape[-1]
    tile_h, tile_w = arrays[0].shape[:2]
    band_h = tile_h * lax.axis_size("rows")
    band_w = tile_w * lax.axis_size("cols")
    up, down, left = shifted("rows", -1), shifted("rows", 1), shifted("cols", -1)

    to_up, to_down, to_corner, to_left = pack(arrays)
    to_left, regions, flip_view = lax.optimization_barrier((to_left, regions, flip_view))
    borrowed = [
        lax.ppermute(to_up, "rows", up),
        lax.ppermute(to_down, "rows", down),
        lax.ppermute(to_corner, ("rows", "cols"), shifted_both(1, -1)),
        lax.ppermute(to_left, "cols", left),
    ]

    row_pos = (lax.axis_index("rows") * tile_h + jnp.arange(tile_h, dtype=jnp.int32) + HALF) % band_h
    col_pos = (lax.axis_index("cols") * tile_w + jnp.arange(tile_w, dtype=jnp.int32) + HALF) % band_w
    key_code = (
        regions[0] * 4
        + (row_pos < HALF).astype(jnp.int32)[:, None] * 2
        + (col_pos < HALF).astype(jnp.int32)[None, :]
    )
    codes = key_code.reshape(2, WIN, 4, WIN).transpose(0, 2, 1, 3)
    codes = jnp.roll(codes, (HALF, HALF), axis=(2, 3)).reshape(2, 4, 1, TOKENS)
    codes_above = lax.ppermute(codes[1, 2:], "rows", down)

    bias = build_bias(bias_table, flip_view[0])

    early, early_sum = attend_early(arrays, codes, out_weight, bias)
    late, to_below, to_above, to_corner, to_right, weight_part = attend_late(
        arrays, borrowed, codes, codes_above, out_weight, bias, early_sum
    )

    home = [
        lax.ppermute(to_below, "rows", down),
        lax.ppermute(to_above, "rows", up),
        lax.ppermute(to_corner, ("rows", "cols"), shifted_both(-1, 1)),
        lax.ppermute(to_right, "cols", shifted("cols", 1)),
    ]
    grads = []

    def between(step, share):
        if step == 5:
            share, *home[:] = lax.optimization_barrier((share, *home))
        if step == 6:
            grads[:] = unpack_all([early, late, *home], width)
            share, *grads[:] = lax.optimization_barrier((share, *grads))
        return share

    weight_total = sum_over_all(weight_part, between)
    factor = jnp.minimum(1.0, clip_norm / jnp.sqrt(jnp.sum(weight_total * weight_total) + 1e-06))
    grad_weight = weight_total * factor
    return (grads[0][None], grads[1][None], grads[2][None], grad_weight)


def solution(mesh):
    return jax.shard_map(
        body,
        mesh=mesh,
        in_specs=(
            P("views", "rows", "cols", None),
            P("views", "rows", "cols", None),
            P("views", "rows", "cols", None),
            P("views", "rows", "cols", None),
            P("views", "rows", "cols"),
            P("views"),
            P(),
            P(),
        ),
        out_specs=(
            P("views", "rows", "cols", None),
            P("views", "rows", "cols", None),
            P("views", "rows", "cols", None),
            P(),
        ),
        check_vma=False,
    )
```

```python
import math

import jax
import jax.numpy as jnp
from jax import lax
from jax.experimental import pallas as pl
from jax.experimental.pallas import tpu as pltpu
from jax.sharding import PartitionSpec as P

HEADS = 12
WIN = 16
HALF = 8
TOKENS = WIN * WIN
HEAD_DIM = 32
LANES = 128
PER_GROUP = LANES // HEAD_DIM
PAIR = 2
VMEM = 60 * 2**20
LOG2E = math.log2(math.e)
SCALING = HEAD_DIM**-0.5
FAR = 1e30
clip_norm = 384.0

f32 = jnp.float32
bf16 = jnp.bfloat16


def bias_kernel(table_ref, bias_ref):
    span = lax.broadcasted_iota(jnp.int32, (32, 512), 1)
    row_hot = (lax.broadcasted_iota(jnp.int32, (32, 512), 0) == 30 - span // WIN).astype(f32)
    col_class = lax.broadcasted_iota(jnp.int32, (WIN, 512), 1) % WIN
    for head in range(PER_GROUP):
        wide = jnp.dot(
            table_ref[head], row_hot, preferred_element_type=f32, precision=lax.Precision.HIGHEST
        ) * LOG2E
        strip = jnp.zeros((WIN, 512), f32)
        for place in range(WIN):
            col = place ^ HALF
            piece = jnp.concatenate([wide[23 - col : 31 - col], wide[15 - col : 23 - col]], axis=0)
            strip = jnp.where(col_class == place, piece, strip)
        for place in range(WIN):
            start = WIN * (15 - (place ^ HALF))
            moved = pltpu.roll(strip, 512 - start, 1) if start else strip
            bias_ref[head, WIN * place : WIN * (place + 1)] = jnp.concatenate(
                [moved[:, LANES : 2 * LANES], moved[:, :LANES]], axis=1
            )


def build_bias(table, code):
    turned = jnp.where(code >= 4, jnp.swapaxes(table, 1, 2), table)
    turned = jnp.where((code // 2) % 2 == 1, turned[:, ::-1], turned)
    turned = jnp.where(code % 2 == 1, turned[:, :, ::-1], turned)
    turned = jnp.pad(jnp.swapaxes(turned, 1, 2), ((0, 0), (0, 1), (0, 1)))
    return pl.pallas_call(
        bias_kernel,
        grid=(HEADS // PER_GROUP,),
        in_specs=[pl.BlockSpec((PER_GROUP, 32, 32), lambda h: (h, 0, 0))],
        out_specs=pl.BlockSpec((PER_GROUP, TOKENS, TOKENS), lambda h: (h, 0, 0)),
        out_shape=jax.ShapeDtypeStruct((HEADS, TOKENS, TOKENS), f32),
        compiler_params=pltpu.CompilerParams(vmem_limit_bytes=VMEM),
        cost_estimate=pl.CostEstimate(flops=10**8, bytes_accessed=4 * 10**6, transcendentals=0),
        name="bias",
    )(turned)


def head_rows(block, j):
    parts = [block[HEAD_DIM * j : HEAD_DIM * (j + 1)]]
    if j > 0:
        parts.insert(0, jnp.zeros((HEAD_DIM * j, TOKENS), bf16))
    if j < PER_GROUP - 1:
        parts.append(jnp.zeros((LANES - HEAD_DIM * (j + 1), TOKENS), bf16))
    return jnp.concatenate(parts, axis=0)


def group_lanes(group):
    return slice(LANES * group, LANES * (group + 1))


def window_pass(cells, code_row, w_ref, bias_refs, store):
    g = cells(3, slice(None))
    hot = (lax.broadcasted_iota(jnp.int32, (LANES, TOKENS), 0) == code_row).astype(f32)
    apart = jnp.concatenate([(hot * -FAR).astype(bf16)] * PAIR, axis=1)
    codes_off = (1.0 - hot).astype(bf16).T
    grad_ctx = lax.dot_general(
        g, w_ref[...], (((1,), (1,)), ((), ())), preferred_element_type=f32
    )
    grad_ctx_t = grad_ctx.astype(bf16).T
    ones = jnp.ones((WIN, TOKENS), bf16)
    lane_head = lax.broadcasted_iota(jnp.int32, (TOKENS, LANES), 1) // HEAD_DIM
    groups, contexts = {}, []

    def open_group(n):
        q, k, v = (cells(i, group_lanes(n)) for i in range(3))
        groups[n] = dict(
            q=q, v=v, q_t=q.T, k_t=k.T, v_t=v.T,
            keys=jnp.concatenate([k, codes_off], axis=1),
            grad_ctx=grad_ctx[:, group_lanes(n)], grad_ctx_t=grad_ctx_t[group_lanes(n)],
            weights=[], scales=[], inners=[], grad_q=[], grad_scores=[],
        )

    def halves(both):
        return [both[:, TOKENS * i : TOKENS * (i + 1)] for i in range(PAIR)]

    def pair_rows(block, j):
        return jnp.concatenate([head_rows(block, j + i) for i in range(PAIR)], axis=1)

    def pair_scores(head):
        part = groups[head // PER_GROUP]
        right = jnp.concatenate([pair_rows(part["q_t"], head % PER_GROUP), apart], axis=0)
        return halves(jnp.dot(part["keys"], right, preferred_element_type=f32))

    def pair_grad_probs(head):
        part = groups[head // PER_GROUP]
        right = pair_rows(part["grad_ctx_t"], head % PER_GROUP)
        return halves(jnp.dot(part["v"], right, preferred_element_type=f32))

    def softmax(head, scores):
        part, j = groups[head // PER_GROUP], head % PER_GROUP
        own = slice(HEAD_DIM * j, HEAD_DIM * (j + 1))
        scores = scores * (LOG2E * SCALING) + bias_refs[head // PER_GROUP][j]
        expd = jnp.exp2(scores - jnp.max(scores, axis=0, keepdims=True)).astype(bf16)
        summed = jnp.dot(
            jnp.concatenate([part["v_t"][own], ones], axis=0), expd, preferred_element_type=f32
        )
        scale = 1.0 / summed[HEAD_DIM : HEAD_DIM + 1]
        context = summed[:HEAD_DIM] * scale
        part["inners"].append(
            jnp.sum(context * part["grad_ctx_t"][own].astype(f32), axis=0, keepdims=True)
        )
        part["weights"].append(expd)
        part["scales"].append(scale)
        contexts.append(context.astype(bf16))

    def score_grads(head, grad_probs):
        part, j = groups[head // PER_GROUP], head % PER_GROUP
        own = slice(HEAD_DIM * j, HEAD_DIM * (j + 1))
        grad_scores = (
            part["weights"][j].astype(f32) * (grad_probs - part["inners"][j])
        ).astype(bf16)
        part["grad_scores"].append(grad_scores)
        part["grad_q"].append(
            jnp.dot(part["k_t"][own], grad_scores, preferred_element_type=f32)
            * (part["scales"][j] * SCALING)
        )

    def stacked_heads(block):
        zero = jnp.zeros_like(block)
        return jnp.concatenate(
            [jnp.where(lane_head == j, block, zero) for j in range(PER_GROUP)], axis=0
        )

    def close_group(n):
        part = groups.pop(n)
        scale_cols = jnp.concatenate(
            [jnp.broadcast_to(scale, (HEAD_DIM, TOKENS)) for scale in part["scales"]], axis=0
        ).T
        q_scaled = (part["q"].astype(f32) * (scale_cols * SCALING)).astype(bf16)
        grad_ctx_scaled = (part["grad_ctx"] * scale_cols).astype(bf16)
        grad_k = jnp.dot(
            jnp.concatenate(part["grad_scores"], axis=1),
            stacked_heads(q_scaled),
            preferred_element_type=f32,
        )
        grad_v = jnp.dot(
            jnp.concatenate(part["weights"], axis=1),
            stacked_heads(grad_ctx_scaled),
            preferred_element_type=f32,
        )
        grad_q = jnp.concatenate(part["grad_q"], axis=0).astype(bf16).T
        store(group_lanes(n), grad_q, grad_k.astype(bf16), grad_v.astype(bf16))

    open_group(0)
    scores, grad_probs = {}, {}
    scores.update(zip(range(PAIR), pair_scores(0)))
    for first in range(0, HEADS + PAIR, PAIR):
        after = first + PAIR
        if after < HEADS:
            if after % PER_GROUP == 0:
                open_group(after // PER_GROUP)
            scores.update(zip(range(after, after + PAIR), pair_scores(after)))
        if first < HEADS:
            grad_probs.update(zip(range(first, after), pair_grad_probs(first)))
        for head in range(first, after):
            if head < HEADS:
                softmax(head, scores.pop(head))
            before = head - PAIR
            if before >= 0:
                score_grads(before, grad_probs.pop(before))
                if before % PER_GROUP == PER_GROUP - 1:
                    close_group(before // PER_GROUP)
    return jnp.dot(jnp.concatenate(contexts, axis=0), g, preferred_element_type=f32)


def merged(low, high):
    place = lax.broadcasted_iota(jnp.int32, low.shape, low.ndim - 2)
    return jnp.where(place < HALF, low, high)


def swapped(tiles):
    wide = tiles.astype(f32)
    return jnp.concatenate([wide[:, HALF:], wide[:, :HALF]], axis=1).astype(bf16)


def pack_low(tiles):
    n = tiles.shape[0] // 2
    return merged(tiles[:n], swapped(tiles[n:]))


def pack_high(tiles):
    n = tiles.shape[0] // 2
    return merged(swapped(tiles[n:]), tiles[:n])


def unpack(tiles):
    return jnp.concatenate([tiles, swapped(tiles)], axis=0)


def tile(ref, t, rows=slice(None)):
    return ref[rows, WIN * t : WIN * (t + 1), :]


def pack_kernel(*refs):
    ins, outs = refs[:12], refs[12:]
    up_ref, down_ref, corner_ref, left_ref = outs
    for i in range(4):
        top, bottom, middle = ins[3 * i : 3 * i + 3]
        for w in range(2):
            up_ref[i, w] = merged(tile(top, w + 1), tile(top, w))
        down_ref[i, :HALF] = merged(tile(bottom, 3), tile(bottom, 2))
        down_ref[i, HALF:] = pack_high(tile(bottom, 3))
        corner_ref[i] = pack_low(tile(bottom, 0))
        left_ref[i] = pack_low(middle[...])


def pack(arrays):
    width = arrays[0].shape[-1]
    top = pl.BlockSpec((HALF, 64, width), lambda i: (0, 0, 0))
    bottom = pl.BlockSpec((HALF, 64, width), lambda i: (3, 0, 0))
    middle = pl.BlockSpec((24, WIN, width), lambda i: (0, 0, 0))
    shapes = [(4, 2, HALF, WIN, width), (4, 12, WIN, width), (4, 4, WIN, width), (4, 12, WIN, width)]
    return pl.pallas_call(
        pack_kernel,
        grid=(1,),
        in_specs=[top, bottom, middle] * 4,
        out_specs=[pl.BlockSpec(s, lambda i, n=len(s): (0,) * n) for s in shapes],
        out_shape=[jax.ShapeDtypeStruct(s, bf16) for s in shapes],
        compiler_params=pltpu.CompilerParams(vmem_limit_bytes=VMEM),
        name="pack",
    )(*[a for a in arrays for _ in range(3)])


def bias_specs():
    return [
        pl.BlockSpec((PER_GROUP, TOKENS, TOKENS), lambda w, n=n: (n, 0, 0))
        for n in range(HEADS // PER_GROUP)
    ]


def early_kernel(*refs):
    tiles, (code_ref, w_ref), bias_refs = refs[:16], refs[16:18], refs[18:21]
    grad_ref, ws_ref, cells_ref = refs[21:]

    @pl.when(pl.program_id(0) == 0)
    def _():
        ws_ref[...] = jnp.zeros_like(ws_ref)

    for i in range(4):
        upper, lower, upper_next, lower_next = (ref[...] for ref in tiles[4 * i : 4 * i + 4])
        cells_ref[i, :HALF] = merged(lower_next, lower)
        cells_ref[i, HALF:] = merged(upper_next, upper)

    def store(lanes, *grads):
        for i, grad in enumerate(grads):
            grad_ref[i, 0, :, :, lanes] = grad.reshape(WIN, WIN, LANES)

    ws_ref[...] += window_pass(
        lambda i, lanes: cells_ref[i, :, :, lanes].reshape(TOKENS, -1), code_ref[0, 0], w_ref, bias_refs, store
    )


def attend_early(arrays, codes, out_weight, bias):
    width = arrays[0].shape[-1]
    corners = [
        pl.BlockSpec((HALF, WIN, width), lambda w, r=r, n=n: (r, w + n, 0))
        for n in (0, 1)
        for r in (1, 2)
    ]
    return pl.pallas_call(
        early_kernel,
        grid=(3,),
        in_specs=corners * 4
        + [
            pl.BlockSpec((1, 1, 1, TOKENS), lambda w: (0, w, 0, 0)),
            pl.BlockSpec((width, width), lambda w: (0, 0)),
        ]
        + bias_specs(),
        out_specs=[
            pl.BlockSpec((3, 1, WIN, WIN, width), lambda w: (0, w, 0, 0, 0)),
            pl.BlockSpec((width, width), lambda w: (0, 0)),
        ],
        out_shape=[
            jax.ShapeDtypeStruct((3, 3, WIN, WIN, width), bf16),
            jax.ShapeDtypeStruct((width, width), f32),
        ],
        scratch_shapes=[pltpu.VMEM((4, WIN, WIN, width), bf16)],
        compiler_params=pltpu.CompilerParams(vmem_limit_bytes=VMEM),
        cost_estimate=pl.CostEstimate(flops=10**10, bytes_accessed=10**7, transcendentals=0),
        name="attend_early",
    )(*[a for a in arrays for _ in range(4)], codes, out_weight, bias, bias, bias)


def late_kernel(*refs):
    parts, refs = refs[:8], refs[8:]
    up_ref, down_ref, corner_ref, left_ref, code_ref, code_above_ref, w_ref, before_ref = refs[:8]
    bias_refs, refs = refs[8:11], refs[11:]
    own_ref, below_ref, above_ref, corner_out_ref, right_ref, ws_ref, cells_ref = refs
    window = pl.program_id(0)

    @pl.when(window == 0)
    def _():
        ws_ref[...] = before_ref[...]

    @pl.when(window < 2)
    def _():
        for i in range(4):
            cells_ref[i, :HALF] = up_ref[i, 0]
            cells_ref[i, HALF:] = merged(parts[2 * i + 1][...], parts[2 * i][...])

    @pl.when(window == 2)
    def _():
        for i in range(4):
            cells_ref[i, :HALF] = merged(parts[2 * i + 1][...], parts[2 * i][...])
            cells_ref[i, HALF:] = down_ref[i, :HALF]

    @pl.when(window == 3)
    def _():
        for i in range(4):
            cells_ref[i, :HALF] = merged(unpack(left_ref[i])[:HALF], parts[2 * i][...])
            cells_ref[i, HALF:] = merged(unpack(corner_ref[i]), unpack(down_ref[i, HALF:]))

    @pl.when(window == 4)
    def _():
        for i in range(4):
            beside = unpack(left_ref[i])
            cells_ref[i, :HALF] = merged(beside[16:], parts[2 * i + 1][...])
            cells_ref[i, HALF:] = merged(beside[8:16], parts[2 * i][...])

    above = (window == 2) | (window == 3)
    code_row = jnp.where(above, code_above_ref[0], code_ref[0, 0])

    def store(lanes, *grads):
        for i, grad in enumerate(grads):
            own_ref[i, 0, :, :, lanes] = grad.reshape(WIN, WIN, LANES)

    ws_ref[...] += window_pass(
        lambda i, lanes: cells_ref[i, :, :, lanes].reshape(TOKENS, -1), code_row, w_ref, bias_refs, store
    )

    for w in range(2):

        @pl.when(window == w)
        def _():
            for i in range(3):
                below_ref[i, w] = own_ref[i, 0, :HALF]

    @pl.when(window == 2)
    def _():
        for i in range(3):
            above_ref[i, :HALF] = own_ref[i, 0, HALF:]

    @pl.when(window == 4)
    def _():
        for i in range(3):
            right_ref[i, 4:] = pack_low(own_ref[i, 0])

    @pl.when(window == 3)
    def _():
        for i in range(3):
            above_ref[i, HALF:] = pack_high(own_ref[i, 0, HALF:])
            corner_out_ref[i] = pack_low(own_ref[i, 0, HALF:])
            right_ref[i, :4] = pack_low(own_ref[i, 0, :HALF])


def attend_late(arrays, borrowed, codes, codes_above, out_weight, bias, before):
    width = arrays[0].shape[-1]
    fixed = lambda shape: pl.BlockSpec(shape, lambda w, n=len(shape): (0,) * n)

    def rows_of(w, side):
        return jnp.where(w < 2, 3, jnp.where(w < 4, 0, 1 + side))

    parts = [
        pl.BlockSpec((HALF, WIN, width), lambda w: (rows_of(w, 0), jnp.minimum(w, 3), 0)),
        pl.BlockSpec((HALF, WIN, width), lambda w: (rows_of(w, 1), jnp.minimum(w + 1, 3), 0)),
    ]
    up_spec = pl.BlockSpec((4, 1, HALF, WIN, width), lambda w: (0, jnp.minimum(w, 1), 0, 0, 0))
    back = [(3, 2, HALF, WIN, width), (3, 12, WIN, width), (3, 4, WIN, width), (3, 12, WIN, width)]
    return pl.pallas_call(
        late_kernel,
        grid=(5,),
        in_specs=parts * 4
        + [up_spec]
        + [fixed(b.shape) for b in borrowed[1:]]
        + [
            pl.BlockSpec(
                (1, 1, 1, TOKENS),
                lambda w: (jnp.where(w < 4, 1, 0), jnp.where(w < 2, w, 3), 0, 0),
            ),
            pl.BlockSpec((1, 1, TOKENS), lambda w: (jnp.where(w == 3, 1, 0), 0, 0)),
            fixed((width, width)),
            fixed((width, width)),
        ]
        + bias_specs(),
        out_specs=[pl.BlockSpec((3, 1, WIN, WIN, width), lambda w: (0, w, 0, 0, 0))]
        + [fixed(s) for s in back]
        + [fixed((width, width))],
        out_shape=[jax.ShapeDtypeStruct((3, 5, WIN, WIN, width), bf16)]
        + [jax.ShapeDtypeStruct(s, bf16) for s in back]
        + [jax.ShapeDtypeStruct((width, width), f32)],
        scratch_shapes=[pltpu.VMEM((4, WIN, WIN, width), bf16)],
        compiler_params=pltpu.CompilerParams(vmem_limit_bytes=VMEM),
        cost_estimate=pl.CostEstimate(flops=2 * 10**10, bytes_accessed=2 * 10**7, transcendentals=0),
        name="attend_late",
    )(
        *[a for a in arrays for _ in range(2)],
        *borrowed,
        codes,
        codes_above,
        out_weight,
        before,
        bias,
        bias,
        bias,
    )


def unpack_kernel(early_ref, late_ref, below_ref, above_ref, corner_ref, left_ref, out):
    left, edge = unpack(left_ref[0, 4:]), unpack(left_ref[0, :4])
    above = unpack(above_ref[0, HALF:])

    def put(half, tiles):
        for t in range(4):
            rows = slice(HALF * half, HALF * (half + 1))
            out[rows, WIN * t : WIN * (t + 1), :] = merged(tiles[t], tiles[t + 1])

    put(0, [edge, below_ref[0, 0], below_ref[0, 1], late_ref[0, 2, :HALF], late_ref[0, 3, :HALF]])
    for half, rows in ((1, slice(HALF, WIN)), (2, slice(0, HALF))):
        own = [early_ref[0, w, rows] for w in range(3)] + [late_ref[0, 4, rows]]
        put(half, [left[rows]] + own)
    put(
        3,
        [unpack(corner_ref[0]), late_ref[0, 0, HALF:], late_ref[0, 1, HALF:], above_ref[0, :HALF], above],
    )


def unpack_one(which, pieces, width):
    out = (32, 64, width)
    return pl.pallas_call(
        unpack_kernel,
        grid=(1,),
        in_specs=[
            pl.BlockSpec((1,) + p.shape[1:], lambda i, n=p.ndim: (which,) + (0,) * (n - 1))
            for p in pieces
        ],
        out_specs=pl.BlockSpec(out, lambda i: (0, 0, 0)),
        out_shape=jax.ShapeDtypeStruct(out, bf16),
        compiler_params=pltpu.CompilerParams(vmem_limit_bytes=VMEM),
        cost_estimate=pl.CostEstimate(flops=10**6, bytes_accessed=3 * 10**6, transcendentals=0),
        name="unpack",
    )(*pieces)


def shifted(axis, distance):
    n = lax.axis_size(axis)
    return [(i, (i + distance) % n) for i in range(n)]


def shifted_both(row_distance, col_distance):
    rows, cols = lax.axis_size("rows"), lax.axis_size("cols")
    return [
        (r * cols + c, (r + row_distance) % rows * cols + (c + col_distance) % cols)
        for r in range(rows)
        for c in range(cols)
    ]


def xor_partners(axis, mask):
    n = 8 if axis == ("cols", "views") else lax.axis_size(axis)
    return [(i, i ^ mask) for i in range(n)]


def sum_over_all(part, between):
    place = lax.axis_index("cols") * 2 + lax.axis_index("views")
    near = ("cols", "views")
    masks = (2, 1, 5)
    labels = (place // 2 % 2, (place ^ place // 4) % 2, place // 4)
    share, bits = part, []
    for mask, bit in zip(masks, labels):
        half = share.shape[0] // 2
        keep = lax.dynamic_slice_in_dim(share, bit * half, half)
        give = lax.dynamic_slice_in_dim(share, (1 - bit) * half, half)
        share = between(len(bits), keep + lax.ppermute(give, near, xor_partners(near, mask)))
        bits.append(bit)
    for step, mask in enumerate((1, 3, 7, 8, 24)):
        share = between(3 + step, share + lax.ppermute(share, "rows", xor_partners("rows", mask)))
    rows, width = share.shape
    rest, parts = jnp.sum(share * share), []
    for _ in range(3):
        parts.append(lax.reduce_precision(rest, 8, 7))
        rest = rest - parts[-1]
    tail = jnp.concatenate(
        [jnp.full((1, width), part, bf16) for part in parts] + [jnp.zeros((WIN - 3, width), bf16)]
    )
    share = jnp.concatenate([share.astype(bf16), tail])
    for mask, bit in zip(masks[::-1], bits[::-1]):
        other = lax.ppermute(share, near, xor_partners(near, mask))
        share = jnp.where(bit == 0, jnp.concatenate([share, other]), jnp.concatenate([other, share]))
    shares = share.reshape(-1, rows + WIN, width).astype(f32)
    return shares[:, :rows].reshape(part.shape), jnp.sum(shares[:, rows : rows + 3, 0])


def body(queries, key_rows, value_rows, grad_out, regions, flip_view, bias_table, out_weight):
    arrays = [array[0] for array in (queries, key_rows, value_rows, grad_out)]
    width = arrays[0].shape[-1]
    tile_h, tile_w = arrays[0].shape[:2]
    band_h = tile_h * lax.axis_size("rows")
    band_w = tile_w * lax.axis_size("cols")
    up, down, left = shifted("rows", -1), shifted("rows", 1), shifted("cols", -1)

    to_up, to_down, to_corner, to_left = pack(arrays)
    to_left, regions, flip_view = lax.optimization_barrier((to_left, regions, flip_view))
    borrowed = [
        lax.ppermute(to_up, "rows", up),
        lax.ppermute(to_down, "rows", down),
        lax.ppermute(to_corner, ("rows", "cols"), shifted_both(1, -1)),
        lax.ppermute(to_left, "cols", left),
    ]

    row_pos = (lax.axis_index("rows") * tile_h + jnp.arange(tile_h, dtype=jnp.int32) + HALF) % band_h
    col_pos = (lax.axis_index("cols") * tile_w + jnp.arange(tile_w, dtype=jnp.int32) + HALF) % band_w
    key_code = (
        regions[0] * 4
        + (row_pos < HALF).astype(jnp.int32)[:, None] * 2
        + (col_pos < HALF).astype(jnp.int32)[None, :]
    )
    codes = key_code.reshape(2, WIN, 4, WIN).transpose(0, 2, 1, 3)
    codes = jnp.roll(codes, (HALF, HALF), axis=(2, 3)).reshape(2, 4, 1, TOKENS)
    codes_above = lax.ppermute(codes[1, 2:], "rows", down)

    bias = build_bias(bias_table, flip_view[0])

    early, early_sum = attend_early(arrays, codes, out_weight, bias)
    late, to_below, to_above, to_corner, to_right, weight_part = attend_late(
        arrays, borrowed, codes, codes_above, out_weight, bias, early_sum
    )

    home = [
        lax.ppermute(to_below, "rows", down),
        lax.ppermute(to_above, "rows", up),
        lax.ppermute(to_corner, ("rows", "cols"), shifted_both(-1, 1)),
        lax.ppermute(to_right, "cols", shifted("cols", 1)),
    ]
    grads = []

    def between(step, share):
        if 3 <= step < 6:
            grads.append(unpack_one(step - 3, [early, late, *home], width))
            share, grads[-1] = lax.optimization_barrier((share, grads[-1]))
        if 2 <= step < 5:
            share, *home[:] = lax.optimization_barrier((share, *home))
        return share

    weight_total, square_sum = sum_over_all(weight_part, between)
    factor = jnp.minimum(1.0, clip_norm / jnp.sqrt(square_sum + 1e-06))
    grad_weight = weight_total * factor
    return (grads[0][None], grads[1][None], grads[2][None], grad_weight)


def solution(mesh):
    return jax.shard_map(
        body,
        mesh=mesh,
        in_specs=(
            P("views", "rows", "cols", None),
            P("views", "rows", "cols", None),
            P("views", "rows", "cols", None),
            P("views", "rows", "cols", None),
            P("views", "rows", "cols"),
            P("views"),
            P(),
            P(),
        ),
        out_specs=(
            P("views", "rows", "cols", None),
            P("views", "rows", "cols", None),
            P("views", "rows", "cols", None),
            P(),
        ),
        check_vma=False,
    )
```

```python
import math

import jax
import jax.numpy as jnp
from jax import lax
from jax.experimental import pallas as pl
from jax.experimental.pallas import tpu as pltpu
from jax.sharding import PartitionSpec as P

HEADS = 12
WIN = 16
HALF = 8
TOKENS = WIN * WIN
HEAD_DIM = 32
LANES = 128
PER_GROUP = LANES // HEAD_DIM
PAIR = 2
VMEM = 60 * 2**20
LOG2E = math.log2(math.e)
SCALING = HEAD_DIM**-0.5
FAR = 1e30
clip_norm = 384.0

f32 = jnp.float32
bf16 = jnp.bfloat16


def bias_kernel(table_ref, bias_ref):
    span = lax.broadcasted_iota(jnp.int32, (32, 512), 1)
    row_hot = (lax.broadcasted_iota(jnp.int32, (32, 512), 0) == 30 - span // WIN).astype(f32)
    col_class = lax.broadcasted_iota(jnp.int32, (WIN, 512), 1) % WIN
    for head in range(PER_GROUP):
        wide = jnp.dot(
            table_ref[head], row_hot, preferred_element_type=f32, precision=lax.Precision.HIGHEST
        ) * LOG2E
        strip = jnp.zeros((WIN, 512), f32)
        for place in range(WIN):
            col = place ^ HALF
            piece = jnp.concatenate([wide[23 - col : 31 - col], wide[15 - col : 23 - col]], axis=0)
            strip = jnp.where(col_class == place, piece, strip)
        for place in range(WIN):
            start = WIN * (15 - (place ^ HALF))
            moved = pltpu.roll(strip, 512 - start, 1) if start else strip
            bias_ref[head, WIN * place : WIN * (place + 1)] = jnp.concatenate(
                [moved[:, LANES : 2 * LANES], moved[:, :LANES]], axis=1
            )


def build_bias(table, code):
    turned = jnp.where(code >= 4, jnp.swapaxes(table, 1, 2), table)
    turned = jnp.where((code // 2) % 2 == 1, turned[:, ::-1], turned)
    turned = jnp.where(code % 2 == 1, turned[:, :, ::-1], turned)
    turned = jnp.pad(jnp.swapaxes(turned, 1, 2), ((0, 0), (0, 1), (0, 1)))
    return pl.pallas_call(
        bias_kernel,
        grid=(HEADS // PER_GROUP,),
        in_specs=[pl.BlockSpec((PER_GROUP, 32, 32), lambda h: (h, 0, 0))],
        out_specs=pl.BlockSpec((PER_GROUP, TOKENS, TOKENS), lambda h: (h, 0, 0)),
        out_shape=jax.ShapeDtypeStruct((HEADS, TOKENS, TOKENS), f32),
        compiler_params=pltpu.CompilerParams(vmem_limit_bytes=VMEM),
        cost_estimate=pl.CostEstimate(flops=10**8, bytes_accessed=4 * 10**6, transcendentals=0),
        name="bias",
    )(turned)


def head_rows(block, j):
    parts = [block[HEAD_DIM * j : HEAD_DIM * (j + 1)]]
    if j > 0:
        parts.insert(0, jnp.zeros((HEAD_DIM * j, TOKENS), bf16))
    if j < PER_GROUP - 1:
        parts.append(jnp.zeros((LANES - HEAD_DIM * (j + 1), TOKENS), bf16))
    return jnp.concatenate(parts, axis=0)


def group_lanes(group):
    return slice(LANES * group, LANES * (group + 1))


def window_pass(cells, code_row, w_ref, bias_refs, store):
    g = cells(3, slice(None))
    hot = (lax.broadcasted_iota(jnp.int32, (LANES, TOKENS), 0) == code_row).astype(f32)
    apart = jnp.concatenate([(hot * -FAR).astype(bf16)] * PAIR, axis=1)
    codes_off = (1.0 - hot).astype(bf16).T
    grad_ctx = lax.dot_general(
        g, w_ref[...], (((1,), (1,)), ((), ())), preferred_element_type=f32
    )
    grad_ctx_t = grad_ctx.astype(bf16).T
    ones = jnp.ones((WIN, TOKENS), bf16)
    lane_head = lax.broadcasted_iota(jnp.int32, (TOKENS, LANES), 1) // HEAD_DIM
    groups, contexts = {}, []

    def open_group(n):
        q, k, v = (cells(i, group_lanes(n)) for i in range(3))
        groups[n] = dict(
            q=q, v=v, q_t=q.T, k_t=k.T, v_t=v.T,
            keys=jnp.concatenate([k, codes_off], axis=1),
            grad_ctx=grad_ctx[:, group_lanes(n)], grad_ctx_t=grad_ctx_t[group_lanes(n)],
            weights=[], scales=[], inners=[], grad_q=[], grad_scores=[],
        )

    def halves(both):
        return [both[:, TOKENS * i : TOKENS * (i + 1)] for i in range(PAIR)]

    def pair_rows(block, j):
        return jnp.concatenate([head_rows(block, j + i) for i in range(PAIR)], axis=1)

    def pair_scores(head):
        part = groups[head // PER_GROUP]
        right = jnp.concatenate([pair_rows(part["q_t"], head % PER_GROUP), apart], axis=0)
        return halves(jnp.dot(part["keys"], right, preferred_element_type=f32))

    def pair_grad_probs(head):
        part = groups[head // PER_GROUP]
        right = pair_rows(part["grad_ctx_t"], head % PER_GROUP)
        return halves(jnp.dot(part["v"], right, preferred_element_type=f32))

    def softmax(head, scores):
        part, j = groups[head // PER_GROUP], head % PER_GROUP
        own = slice(HEAD_DIM * j, HEAD_DIM * (j + 1))
        scores = scores * (LOG2E * SCALING) + bias_refs[head // PER_GROUP][j]
        expd = jnp.exp2(scores - jnp.max(scores, axis=0, keepdims=True)).astype(bf16)
        summed = jnp.dot(
            jnp.concatenate([part["v_t"][own], ones], axis=0), expd, preferred_element_type=f32
        )
        scale = 1.0 / summed[HEAD_DIM : HEAD_DIM + 1]
        context = summed[:HEAD_DIM] * scale
        part["inners"].append(
            jnp.sum(context * part["grad_ctx_t"][own].astype(f32), axis=0, keepdims=True)
        )
        part["weights"].append(expd)
        part["scales"].append(scale)
        contexts.append(context.astype(bf16))

    def score_grads(head, grad_probs):
        part, j = groups[head // PER_GROUP], head % PER_GROUP
        own = slice(HEAD_DIM * j, HEAD_DIM * (j + 1))
        grad_scores = (
            part["weights"][j].astype(f32) * (grad_probs - part["inners"][j])
        ).astype(bf16)
        part["grad_scores"].append(grad_scores)
        part["grad_q"].append(
            jnp.dot(part["k_t"][own], grad_scores, preferred_element_type=f32)
            * (part["scales"][j] * SCALING)
        )

    def stacked_heads(block):
        zero = jnp.zeros_like(block)
        return jnp.concatenate(
            [jnp.where(lane_head == j, block, zero) for j in range(PER_GROUP)], axis=0
        )

    def close_group(n):
        part = groups.pop(n)
        scale_cols = jnp.concatenate(
            [jnp.broadcast_to(scale, (HEAD_DIM, TOKENS)) for scale in part["scales"]], axis=0
        ).T
        q_scaled = (part["q"].astype(f32) * (scale_cols * SCALING)).astype(bf16)
        grad_ctx_scaled = (part["grad_ctx"] * scale_cols).astype(bf16)
        grad_k = jnp.dot(
            jnp.concatenate(part["grad_scores"], axis=1),
            stacked_heads(q_scaled),
            preferred_element_type=f32,
        )
        grad_v = jnp.dot(
            jnp.concatenate(part["weights"], axis=1),
            stacked_heads(grad_ctx_scaled),
            preferred_element_type=f32,
        )
        grad_q = jnp.concatenate(part["grad_q"], axis=0).astype(bf16).T
        store(group_lanes(n), grad_q, grad_k.astype(bf16), grad_v.astype(bf16))

    open_group(0)
    scores, grad_probs = {}, {}
    scores.update(zip(range(PAIR), pair_scores(0)))
    for first in range(0, HEADS + PAIR, PAIR):
        after = first + PAIR
        if after < HEADS:
            if after % PER_GROUP == 0:
                open_group(after // PER_GROUP)
            scores.update(zip(range(after, after + PAIR), pair_scores(after)))
        if first < HEADS:
            grad_probs.update(zip(range(first, after), pair_grad_probs(first)))
        for head in range(first, after):
            if head < HEADS:
                softmax(head, scores.pop(head))
            before = head - PAIR
            if before >= 0:
                score_grads(before, grad_probs.pop(before))
                if before % PER_GROUP == PER_GROUP - 1:
                    close_group(before // PER_GROUP)
    return jnp.dot(jnp.concatenate(contexts, axis=0), g, preferred_element_type=f32)


def merged(low, high):
    place = lax.broadcasted_iota(jnp.int32, low.shape, low.ndim - 2)
    return jnp.where(place < HALF, low, high)


def swapped(tiles):
    wide = tiles.astype(f32)
    return jnp.concatenate([wide[:, HALF:], wide[:, :HALF]], axis=1).astype(bf16)


def pack_low(tiles):
    n = tiles.shape[0] // 2
    return merged(tiles[:n], swapped(tiles[n:]))


def pack_high(tiles):
    n = tiles.shape[0] // 2
    return merged(swapped(tiles[n:]), tiles[:n])


def unpack(tiles):
    return jnp.concatenate([tiles, swapped(tiles)], axis=0)


def tile(ref, t, rows=slice(None)):
    return ref[rows, WIN * t : WIN * (t + 1), :]


def pack_kernel(*refs):
    ins, outs = refs[:12], refs[12:]
    up_ref, down_ref, corner_ref, left_ref = outs
    for i in range(4):
        top, bottom, middle = ins[3 * i : 3 * i + 3]
        for w in range(2):
            up_ref[i, w] = merged(tile(top, w + 1), tile(top, w))
        down_ref[i, :HALF] = merged(tile(bottom, 3), tile(bottom, 2))
        down_ref[i, HALF:] = pack_high(tile(bottom, 3))
        corner_ref[i] = pack_low(tile(bottom, 0))
        left_ref[i] = pack_low(middle[...])


def pack(arrays):
    width = arrays[0].shape[-1]
    top = pl.BlockSpec((HALF, 64, width), lambda i: (0, 0, 0))
    bottom = pl.BlockSpec((HALF, 64, width), lambda i: (3, 0, 0))
    middle = pl.BlockSpec((24, WIN, width), lambda i: (0, 0, 0))
    shapes = [(4, 2, HALF, WIN, width), (4, 12, WIN, width), (4, 4, WIN, width), (4, 12, WIN, width)]
    return pl.pallas_call(
        pack_kernel,
        grid=(1,),
        in_specs=[top, bottom, middle] * 4,
        out_specs=[pl.BlockSpec(s, lambda i, n=len(s): (0,) * n) for s in shapes],
        out_shape=[jax.ShapeDtypeStruct(s, bf16) for s in shapes],
        compiler_params=pltpu.CompilerParams(vmem_limit_bytes=VMEM),
        name="pack",
    )(*[a for a in arrays for _ in range(3)])


def bias_specs():
    return [
        pl.BlockSpec((PER_GROUP, TOKENS, TOKENS), lambda w, n=n: (n, 0, 0))
        for n in range(HEADS // PER_GROUP)
    ]


def early_kernel(*refs):
    tiles, (code_ref, w_ref), bias_refs = refs[:16], refs[16:18], refs[18:21]
    grad_ref, ws_ref, cells_ref = refs[21:]

    @pl.when(pl.program_id(0) == 0)
    def _():
        ws_ref[...] = jnp.zeros_like(ws_ref)

    for i in range(4):
        upper, lower, upper_next, lower_next = (ref[...] for ref in tiles[4 * i : 4 * i + 4])
        cells_ref[i, :HALF] = merged(lower_next, lower)
        cells_ref[i, HALF:] = merged(upper_next, upper)

    def store(lanes, *grads):
        for i, grad in enumerate(grads):
            grad_ref[i, 0, :, :, lanes] = grad.reshape(WIN, WIN, LANES)

    ws_ref[...] += window_pass(
        lambda i, lanes: cells_ref[i, :, :, lanes].reshape(TOKENS, -1), code_ref[0, 0], w_ref, bias_refs, store
    )


def attend_early(arrays, codes, out_weight, bias):
    width = arrays[0].shape[-1]
    corners = [
        pl.BlockSpec((HALF, WIN, width), lambda w, r=r, n=n: (r, w + n, 0))
        for n in (0, 1)
        for r in (1, 2)
    ]
    return pl.pallas_call(
        early_kernel,
        grid=(3,),
        in_specs=corners * 4
        + [
            pl.BlockSpec((1, 1, 1, TOKENS), lambda w: (0, w, 0, 0)),
            pl.BlockSpec((width, width), lambda w: (0, 0)),
        ]
        + bias_specs(),
        out_specs=[
            pl.BlockSpec((3, 1, WIN, WIN, width), lambda w: (0, w, 0, 0, 0)),
            pl.BlockSpec((width, width), lambda w: (0, 0)),
        ],
        out_shape=[
            jax.ShapeDtypeStruct((3, 3, WIN, WIN, width), bf16),
            jax.ShapeDtypeStruct((width, width), f32),
        ],
        scratch_shapes=[pltpu.VMEM((4, WIN, WIN, width), bf16)],
        compiler_params=pltpu.CompilerParams(vmem_limit_bytes=VMEM),
        cost_estimate=pl.CostEstimate(flops=10**10, bytes_accessed=10**7, transcendentals=0),
        name="attend_early",
    )(*[a for a in arrays for _ in range(4)], codes, out_weight, bias, bias, bias)


def late_kernel(*refs):
    parts, refs = refs[:8], refs[8:]
    up_ref, down_ref, corner_ref, left_ref, code_ref, code_above_ref, w_ref, before_ref = refs[:8]
    bias_refs, half_ref, refs = refs[8:11], refs[11], refs[12:]
    own_ref, below_ref, above_ref, corner_out_ref, right_ref, keep_ref, give_ref, cells_ref, ws_ref = refs
    window = pl.program_id(0)

    @pl.when(window == 0)
    def _():
        ws_ref[...] = before_ref[...]

    @pl.when(window < 2)
    def _():
        for i in range(4):
            cells_ref[i, :HALF] = up_ref[i, 0]
            cells_ref[i, HALF:] = merged(parts[2 * i + 1][...], parts[2 * i][...])

    @pl.when(window == 2)
    def _():
        for i in range(4):
            cells_ref[i, :HALF] = merged(parts[2 * i + 1][...], parts[2 * i][...])
            cells_ref[i, HALF:] = down_ref[i, :HALF]

    @pl.when(window == 3)
    def _():
        for i in range(4):
            cells_ref[i, :HALF] = merged(unpack(left_ref[i])[:HALF], parts[2 * i][...])
            cells_ref[i, HALF:] = merged(unpack(corner_ref[i]), unpack(down_ref[i, HALF:]))

    @pl.when(window == 4)
    def _():
        for i in range(4):
            beside = unpack(left_ref[i])
            cells_ref[i, :HALF] = merged(beside[16:], parts[2 * i + 1][...])
            cells_ref[i, HALF:] = merged(beside[8:16], parts[2 * i][...])

    above = (window == 2) | (window == 3)
    code_row = jnp.where(above, code_above_ref[0], code_ref[0, 0])

    def store(lanes, *grads):
        for i, grad in enumerate(grads):
            own_ref[i, 0, :, :, lanes] = grad.reshape(WIN, WIN, LANES)

    ws_ref[...] += window_pass(
        lambda i, lanes: cells_ref[i, :, :, lanes].reshape(TOKENS, -1), code_row, w_ref, bias_refs, store
    )

    for w in range(2):

        @pl.when(window == w)
        def _():
            for i in range(3):
                below_ref[i, w] = own_ref[i, 0, :HALF]

    @pl.when(window == 2)
    def _():
        for i in range(3):
            above_ref[i, :HALF] = own_ref[i, 0, HALF:]

    @pl.when(window == 4)
    def _():
        for i in range(3):
            right_ref[i, 4:] = pack_low(own_ref[i, 0])
        rows = keep_ref.shape[0]
        keep_ref[...] = ws_ref[pl.ds(pl.multiple_of(half_ref[0] * rows, 8), rows)]
        give_ref[...] = ws_ref[pl.ds(pl.multiple_of((1 - half_ref[0]) * rows, 8), rows)]

    @pl.when(window == 3)
    def _():
        for i in range(3):
            above_ref[i, HALF:] = pack_high(own_ref[i, 0, HALF:])
            corner_out_ref[i] = pack_low(own_ref[i, 0, HALF:])
            right_ref[i, :4] = pack_low(own_ref[i, 0, :HALF])


def attend_late(arrays, borrowed, codes, codes_above, out_weight, bias, before, half):
    width = arrays[0].shape[-1]
    fixed = lambda shape: pl.BlockSpec(shape, lambda w, n=len(shape): (0,) * n)

    def rows_of(w, side):
        return jnp.where(w < 2, 3, jnp.where(w < 4, 0, 1 + side))

    parts = [
        pl.BlockSpec((HALF, WIN, width), lambda w: (rows_of(w, 0), jnp.minimum(w, 3), 0)),
        pl.BlockSpec((HALF, WIN, width), lambda w: (rows_of(w, 1), jnp.minimum(w + 1, 3), 0)),
    ]
    up_spec = pl.BlockSpec((4, 1, HALF, WIN, width), lambda w: (0, jnp.minimum(w, 1), 0, 0, 0))
    back = [(3, 2, HALF, WIN, width), (3, 12, WIN, width), (3, 4, WIN, width), (3, 12, WIN, width)]
    return pl.pallas_call(
        late_kernel,
        grid=(5,),
        in_specs=parts * 4
        + [up_spec]
        + [fixed(b.shape) for b in borrowed[1:]]
        + [
            pl.BlockSpec(
                (1, 1, 1, TOKENS),
                lambda w: (jnp.where(w < 4, 1, 0), jnp.where(w < 2, w, 3), 0, 0),
            ),
            pl.BlockSpec((1, 1, TOKENS), lambda w: (jnp.where(w == 3, 1, 0), 0, 0)),
            fixed((width, width)),
            fixed((width, width)),
        ]
        + bias_specs()
        + [pl.BlockSpec(memory_space=pltpu.SMEM)],
        out_specs=[pl.BlockSpec((3, 1, WIN, WIN, width), lambda w: (0, w, 0, 0, 0))]
        + [fixed(s) for s in back]
        + [fixed((width // 2, width))] * 2,
        out_shape=[jax.ShapeDtypeStruct((3, 5, WIN, WIN, width), bf16)]
        + [jax.ShapeDtypeStruct(s, bf16) for s in back]
        + [jax.ShapeDtypeStruct((width // 2, width), f32)] * 2,
        scratch_shapes=[
            pltpu.VMEM((4, WIN, WIN, width), bf16),
            pltpu.VMEM((width, width), f32),
        ],
        compiler_params=pltpu.CompilerParams(vmem_limit_bytes=VMEM),
        cost_estimate=pl.CostEstimate(flops=2 * 10**10, bytes_accessed=2 * 10**7, transcendentals=0),
        name="attend_late",
    )(
        *[a for a in arrays for _ in range(2)],
        *borrowed,
        codes,
        codes_above,
        out_weight,
        before,
        bias,
        bias,
        bias,
        half,
    )


def unpack_kernel(early_ref, late_ref, below_ref, above_ref, corner_ref, left_ref, out):
    left, edge = unpack(left_ref[0, 4:]), unpack(left_ref[0, :4])
    above = unpack(above_ref[0, HALF:])

    def put(half, tiles):
        for t in range(4):
            rows = slice(HALF * half, HALF * (half + 1))
            out[rows, WIN * t : WIN * (t + 1), :] = merged(tiles[t], tiles[t + 1])

    put(0, [edge, below_ref[0, 0], below_ref[0, 1], late_ref[0, 2, :HALF], late_ref[0, 3, :HALF]])
    for half, rows in ((1, slice(HALF, WIN)), (2, slice(0, HALF))):
        own = [early_ref[0, w, rows] for w in range(3)] + [late_ref[0, 4, rows]]
        put(half, [left[rows]] + own)
    put(
        3,
        [unpack(corner_ref[0]), late_ref[0, 0, HALF:], late_ref[0, 1, HALF:], above_ref[0, :HALF], above],
    )


def unpack_one(which, pieces, width):
    out = (32, 64, width)
    return pl.pallas_call(
        unpack_kernel,
        grid=(1,),
        in_specs=[
            pl.BlockSpec((1,) + p.shape[1:], lambda i, n=p.ndim: (which,) + (0,) * (n - 1))
            for p in pieces
        ],
        out_specs=pl.BlockSpec(out, lambda i: (0, 0, 0)),
        out_shape=jax.ShapeDtypeStruct(out, bf16),
        compiler_params=pltpu.CompilerParams(vmem_limit_bytes=VMEM),
        cost_estimate=pl.CostEstimate(flops=10**6, bytes_accessed=3 * 10**6, transcendentals=0),
        name="unpack",
    )(*pieces)


def shifted(axis, distance):
    n = lax.axis_size(axis)
    return [(i, (i + distance) % n) for i in range(n)]


def shifted_both(row_distance, col_distance):
    rows, cols = lax.axis_size("rows"), lax.axis_size("cols")
    return [
        (r * cols + c, (r + row_distance) % rows * cols + (c + col_distance) % cols)
        for r in range(rows)
        for c in range(cols)
    ]


def xor_partners(axis, mask):
    n = 8 if axis == ("cols", "views") else lax.axis_size(axis)
    return [(i, i ^ mask) for i in range(n)]


def sum_over_all(keep, give, between):
    place = lax.axis_index("cols") * 2 + lax.axis_index("views")
    near = ("cols", "views")
    masks = (2, 1, 5)
    labels = (place // 2 % 2, (place ^ place // 4) % 2, place // 4)
    share = between(0, keep + lax.ppermute(give, near, xor_partners(near, masks[0])))
    for step in (1, 2):
        half = share.shape[0] // 2
        keep = lax.dynamic_slice_in_dim(share, labels[step] * half, half)
        give = lax.dynamic_slice_in_dim(share, (1 - labels[step]) * half, half)
        share = between(step, keep + lax.ppermute(give, near, xor_partners(near, masks[step])))
    for step, mask in enumerate((8, 24, 1, 3, 7)):
        share = between(3 + step, share + lax.ppermute(share, "rows", xor_partners("rows", mask)))
    share = share.astype(bf16)
    for mask, bit in zip(masks[::-1], labels[::-1]):
        other = lax.ppermute(share, near, xor_partners(near, mask))
        share = jnp.where(bit == 0, jnp.concatenate([share, other]), jnp.concatenate([other, share]))
    return share.astype(f32)


def body(queries, key_rows, value_rows, grad_out, regions, flip_view, bias_table, out_weight):
    arrays = [array[0] for array in (queries, key_rows, value_rows, grad_out)]
    width = arrays[0].shape[-1]
    tile_h, tile_w = arrays[0].shape[:2]
    band_h = tile_h * lax.axis_size("rows")
    band_w = tile_w * lax.axis_size("cols")
    up, down, left = shifted("rows", -1), shifted("rows", 1), shifted("cols", -1)

    to_up, to_down, to_corner, to_left = pack(arrays)
    to_left, regions, flip_view = lax.optimization_barrier((to_left, regions, flip_view))
    borrowed = [
        lax.ppermute(to_up, "rows", up),
        lax.ppermute(to_down, "rows", down),
        lax.ppermute(to_corner, ("rows", "cols"), shifted_both(1, -1)),
        lax.ppermute(to_left, "cols", left),
    ]

    row_pos = (lax.axis_index("rows") * tile_h + jnp.arange(tile_h, dtype=jnp.int32) + HALF) % band_h
    col_pos = (lax.axis_index("cols") * tile_w + jnp.arange(tile_w, dtype=jnp.int32) + HALF) % band_w
    key_code = (
        regions[0] * 4
        + (row_pos < HALF).astype(jnp.int32)[:, None] * 2
        + (col_pos < HALF).astype(jnp.int32)[None, :]
    )
    codes = key_code.reshape(2, WIN, 4, WIN).transpose(0, 2, 1, 3)
    codes = jnp.roll(codes, (HALF, HALF), axis=(2, 3)).reshape(2, 4, 1, TOKENS)
    codes_above = lax.ppermute(codes[1, 2:], "rows", down)

    bias = build_bias(bias_table, flip_view[0])

    early, early_sum = attend_early(arrays, codes, out_weight, bias)
    core = lax.axis_index("cols") % 2
    late, to_below, to_above, to_corner, to_right, keep, give = attend_late(
        arrays, borrowed, codes, codes_above, out_weight, bias, early_sum, core[None]
    )

    home = [
        lax.ppermute(to_below, "rows", down),
        lax.ppermute(to_above, "rows", up),
        lax.ppermute(to_corner, ("rows", "cols"), shifted_both(-1, 1)),
        lax.ppermute(to_right, "cols", shifted("cols", 1)),
    ]
    grads = []

    def between(step, share):
        if step == 3:
            share, *home[:2] = lax.optimization_barrier((share, *home[:2]))
        if step >= 5:
            grads.append(unpack_one(step - 5, [early, late, *home], width))
            share, grads[-1] = lax.optimization_barrier((share, grads[-1]))
        if 4 <= step < 7:
            share, *home[:] = lax.optimization_barrier((share, *home))
        return share

    weight_total = sum_over_all(keep, give, between)
    factor = jnp.minimum(1.0, clip_norm / jnp.sqrt(jnp.sum(weight_total * weight_total) + 1e-06))
    grad_weight = weight_total * factor
    return (grads[0][None], grads[1][None], grads[2][None], grad_weight)


def solution(mesh):
    return jax.shard_map(
        body,
        mesh=mesh,
        in_specs=(
            P("views", "rows", "cols", None),
            P("views", "rows", "cols", None),
            P("views", "rows", "cols", None),
            P("views", "rows", "cols", None),
            P("views", "rows", "cols"),
            P("views"),
            P(),
            P(),
        ),
        out_specs=(
            P("views", "rows", "cols", None),
            P("views", "rows", "cols", None),
            P("views", "rows", "cols", None),
            P(),
        ),
        check_vma=False,
    )
```

```python
import math

import jax
import jax.numpy as jnp
from jax import lax
from jax.experimental import pallas as pl
from jax.experimental.pallas import tpu as pltpu
from jax.sharding import PartitionSpec as P

HEADS = 12
WIN = 16
HALF = 8
TOKENS = WIN * WIN
HEAD_DIM = 32
LANES = 128
PER_GROUP = LANES // HEAD_DIM
PAIR = 2
VMEM = 60 * 2**20
LOG2E = math.log2(math.e)
SCALING = HEAD_DIM**-0.5
FAR = 1e30
clip_norm = 384.0

f32 = jnp.float32
bf16 = jnp.bfloat16


def bias_kernel(table_ref, bias_ref):
    span = lax.broadcasted_iota(jnp.int32, (32, 512), 1)
    row_hot = (lax.broadcasted_iota(jnp.int32, (32, 512), 0) == 30 - span // WIN).astype(f32)
    col_class = lax.broadcasted_iota(jnp.int32, (WIN, 512), 1) % WIN
    for head in range(PER_GROUP):
        wide = jnp.dot(
            table_ref[head], row_hot, preferred_element_type=f32, precision=lax.Precision.HIGHEST
        ) * LOG2E
        strip = jnp.zeros((WIN, 512), f32)
        for place in range(WIN):
            col = place ^ HALF
            piece = jnp.concatenate([wide[23 - col : 31 - col], wide[15 - col : 23 - col]], axis=0)
            strip = jnp.where(col_class == place, piece, strip)
        for place in range(WIN):
            start = WIN * (15 - (place ^ HALF))
            moved = pltpu.roll(strip, 512 - start, 1) if start else strip
            bias_ref[head, WIN * place : WIN * (place + 1)] = jnp.concatenate(
                [moved[:, LANES : 2 * LANES], moved[:, :LANES]], axis=1
            )


def build_bias(table, code):
    turned = jnp.where(code >= 4, jnp.swapaxes(table, 1, 2), table)
    turned = jnp.where((code // 2) % 2 == 1, turned[:, ::-1], turned)
    turned = jnp.where(code % 2 == 1, turned[:, :, ::-1], turned)
    turned = jnp.pad(jnp.swapaxes(turned, 1, 2), ((0, 0), (0, 1), (0, 1)))
    return pl.pallas_call(
        bias_kernel,
        grid=(HEADS // PER_GROUP,),
        in_specs=[pl.BlockSpec((PER_GROUP, 32, 32), lambda h: (h, 0, 0))],
        out_specs=pl.BlockSpec((PER_GROUP, TOKENS, TOKENS), lambda h: (h, 0, 0)),
        out_shape=jax.ShapeDtypeStruct((HEADS, TOKENS, TOKENS), f32),
        compiler_params=pltpu.CompilerParams(vmem_limit_bytes=VMEM),
        cost_estimate=pl.CostEstimate(flops=10**8, bytes_accessed=4 * 10**6, transcendentals=0),
        name="bias",
    )(turned)


def head_rows(block, j):
    parts = [block[HEAD_DIM * j : HEAD_DIM * (j + 1)]]
    if j > 0:
        parts.insert(0, jnp.zeros((HEAD_DIM * j, TOKENS), bf16))
    if j < PER_GROUP - 1:
        parts.append(jnp.zeros((LANES - HEAD_DIM * (j + 1), TOKENS), bf16))
    return jnp.concatenate(parts, axis=0)


def group_lanes(group):
    return slice(LANES * group, LANES * (group + 1))


def window_pass(cells, code_row, w_ref, bias_refs, store):
    g = cells(3, slice(None))
    hot = (lax.broadcasted_iota(jnp.int32, (LANES, TOKENS), 0) == code_row).astype(f32)
    apart = jnp.concatenate([(hot * -FAR).astype(bf16)] * PAIR, axis=1)
    codes_off = (1.0 - hot).astype(bf16).T
    grad_ctx = lax.dot_general(
        g, w_ref[...], (((1,), (1,)), ((), ())), preferred_element_type=f32
    )
    grad_ctx_t = grad_ctx.astype(bf16).T
    ones = jnp.ones((WIN, TOKENS), bf16)
    lane_head = lax.broadcasted_iota(jnp.int32, (TOKENS, LANES), 1) // HEAD_DIM
    groups, contexts = {}, []

    def open_group(n):
        q, k, v = (cells(i, group_lanes(n)) for i in range(3))
        groups[n] = dict(
            q=q, v=v, q_t=q.T, k_t=k.T, v_t=v.T,
            keys=jnp.concatenate([k, codes_off], axis=1),
            grad_ctx=grad_ctx[:, group_lanes(n)], grad_ctx_t=grad_ctx_t[group_lanes(n)],
            weights=[], scales=[], inners=[], grad_q=[], grad_scores=[],
        )

    def halves(both):
        return [both[:, TOKENS * i : TOKENS * (i + 1)] for i in range(PAIR)]

    def pair_rows(block, j):
        return jnp.concatenate([head_rows(block, j + i) for i in range(PAIR)], axis=1)

    def pair_scores(head):
        part = groups[head // PER_GROUP]
        right = jnp.concatenate([pair_rows(part["q_t"], head % PER_GROUP), apart], axis=0)
        return halves(jnp.dot(part["keys"], right, preferred_element_type=f32))

    def pair_grad_probs(head):
        part = groups[head // PER_GROUP]
        right = pair_rows(part["grad_ctx_t"], head % PER_GROUP)
        return halves(jnp.dot(part["v"], right, preferred_element_type=f32))

    def softmax(head, scores):
        part, j = groups[head // PER_GROUP], head % PER_GROUP
        own = slice(HEAD_DIM * j, HEAD_DIM * (j + 1))
        scores = scores * (LOG2E * SCALING) + bias_refs[head // PER_GROUP][j]
        expd = jnp.exp2(scores - jnp.max(scores, axis=0, keepdims=True)).astype(bf16)
        summed = jnp.dot(
            jnp.concatenate([part["v_t"][own], ones], axis=0), expd, preferred_element_type=f32
        )
        scale = 1.0 / summed[HEAD_DIM : HEAD_DIM + 1]
        context = summed[:HEAD_DIM] * scale
        part["inners"].append(
            jnp.sum(context * part["grad_ctx_t"][own].astype(f32), axis=0, keepdims=True)
        )
        part["weights"].append(expd)
        part["scales"].append(scale)
        contexts.append(context.astype(bf16))

    def score_grads(head, grad_probs):
        part, j = groups[head // PER_GROUP], head % PER_GROUP
        own = slice(HEAD_DIM * j, HEAD_DIM * (j + 1))
        grad_scores = (
            part["weights"][j].astype(f32) * (grad_probs - part["inners"][j])
        ).astype(bf16)
        part["grad_scores"].append(grad_scores)
        part["grad_q"].append(
            jnp.dot(part["k_t"][own], grad_scores, preferred_element_type=f32)
            * (part["scales"][j] * SCALING)
        )

    def stacked_heads(block):
        zero = jnp.zeros_like(block)
        return jnp.concatenate(
            [jnp.where(lane_head == j, block, zero) for j in range(PER_GROUP)], axis=0
        )

    def close_group(n):
        part = groups.pop(n)
        scale_cols = jnp.concatenate(
            [jnp.broadcast_to(scale, (HEAD_DIM, TOKENS)) for scale in part["scales"]], axis=0
        ).T
        q_scaled = (part["q"].astype(f32) * (scale_cols * SCALING)).astype(bf16)
        grad_ctx_scaled = (part["grad_ctx"] * scale_cols).astype(bf16)
        grad_k = jnp.dot(
            jnp.concatenate(part["grad_scores"], axis=1),
            stacked_heads(q_scaled),
            preferred_element_type=f32,
        )
        grad_v = jnp.dot(
            jnp.concatenate(part["weights"], axis=1),
            stacked_heads(grad_ctx_scaled),
            preferred_element_type=f32,
        )
        grad_q = jnp.concatenate(part["grad_q"], axis=0).astype(bf16).T
        store(group_lanes(n), grad_q, grad_k.astype(bf16), grad_v.astype(bf16))

    open_group(0)
    scores, grad_probs = {}, {}
    scores.update(zip(range(PAIR), pair_scores(0)))
    for first in range(0, HEADS + PAIR, PAIR):
        after = first + PAIR
        if after < HEADS:
            if after % PER_GROUP == 0:
                open_group(after // PER_GROUP)
            scores.update(zip(range(after, after + PAIR), pair_scores(after)))
        if first < HEADS:
            grad_probs.update(zip(range(first, after), pair_grad_probs(first)))
        for head in range(first, after):
            if head < HEADS:
                softmax(head, scores.pop(head))
            before = head - PAIR
            if before >= 0:
                score_grads(before, grad_probs.pop(before))
                if before % PER_GROUP == PER_GROUP - 1:
                    close_group(before // PER_GROUP)
    return jnp.dot(jnp.concatenate(contexts, axis=0), g, preferred_element_type=f32)


def merged(low, high):
    place = lax.broadcasted_iota(jnp.int32, low.shape, low.ndim - 2)
    return jnp.where(place < HALF, low, high)


def swapped(tiles):
    wide = tiles.astype(f32)
    return jnp.concatenate([wide[:, HALF:], wide[:, :HALF]], axis=1).astype(bf16)


def pack_low(tiles):
    n = tiles.shape[0] // 2
    return merged(tiles[:n], swapped(tiles[n:]))


def pack_high(tiles):
    n = tiles.shape[0] // 2
    return merged(swapped(tiles[n:]), tiles[:n])


def unpack(tiles):
    return jnp.concatenate([tiles, swapped(tiles)], axis=0)


def tile(ref, t, rows=slice(None)):
    return ref[rows, WIN * t : WIN * (t + 1), :]


def pack_kernel(*refs):
    ins, outs = refs[:12], refs[12:]
    up_ref, down_ref, corner_ref, left_ref = outs
    for i in range(4):
        top, bottom, middle = ins[3 * i : 3 * i + 3]
        for w in range(2):
            up_ref[i, w] = merged(tile(top, w + 1), tile(top, w))
        down_ref[i, :HALF] = merged(tile(bottom, 3), tile(bottom, 2))
        down_ref[i, HALF:] = pack_high(tile(bottom, 3))
        corner_ref[i] = pack_low(tile(bottom, 0))
        left_ref[i] = pack_low(middle[...])


def pack(arrays):
    width = arrays[0].shape[-1]
    top = pl.BlockSpec((HALF, 64, width), lambda i: (0, 0, 0))
    bottom = pl.BlockSpec((HALF, 64, width), lambda i: (3, 0, 0))
    middle = pl.BlockSpec((24, WIN, width), lambda i: (0, 0, 0))
    shapes = [(4, 2, HALF, WIN, width), (4, 12, WIN, width), (4, 4, WIN, width), (4, 12, WIN, width)]
    return pl.pallas_call(
        pack_kernel,
        grid=(1,),
        in_specs=[top, bottom, middle] * 4,
        out_specs=[pl.BlockSpec(s, lambda i, n=len(s): (0,) * n) for s in shapes],
        out_shape=[jax.ShapeDtypeStruct(s, bf16) for s in shapes],
        compiler_params=pltpu.CompilerParams(vmem_limit_bytes=VMEM),
        name="pack",
    )(*[a for a in arrays for _ in range(3)])


def bias_specs():
    return [
        pl.BlockSpec((PER_GROUP, TOKENS, TOKENS), lambda w, n=n: (n, 0, 0))
        for n in range(HEADS // PER_GROUP)
    ]


def early_kernel(*refs):
    tiles, (code_ref, w_ref), bias_refs = refs[:16], refs[16:18], refs[18:21]
    grad_ref, ws_ref, cells_ref = refs[21:]

    @pl.when(pl.program_id(0) == 0)
    def _():
        ws_ref[...] = jnp.zeros_like(ws_ref)

    for i in range(4):
        upper, lower, upper_next, lower_next = (ref[...] for ref in tiles[4 * i : 4 * i + 4])
        cells_ref[i, :HALF] = merged(lower_next, lower)
        cells_ref[i, HALF:] = merged(upper_next, upper)

    def store(lanes, *grads):
        for i, grad in enumerate(grads):
            grad_ref[i, 0, :, :, lanes] = grad.reshape(WIN, WIN, LANES)

    ws_ref[...] += window_pass(
        lambda i, lanes: cells_ref[i, :, :, lanes].reshape(TOKENS, -1), code_ref[0, 0], w_ref, bias_refs, store
    )


def attend_early(arrays, codes, out_weight, bias):
    width = arrays[0].shape[-1]
    corners = [
        pl.BlockSpec((HALF, WIN, width), lambda w, r=r, n=n: (r, w + n, 0))
        for n in (0, 1)
        for r in (1, 2)
    ]
    return pl.pallas_call(
        early_kernel,
        grid=(3,),
        in_specs=corners * 4
        + [
            pl.BlockSpec((1, 1, 1, TOKENS), lambda w: (0, w, 0, 0)),
            pl.BlockSpec((width, width), lambda w: (0, 0)),
        ]
        + bias_specs(),
        out_specs=[
            pl.BlockSpec((3, 1, WIN, WIN, width), lambda w: (0, w, 0, 0, 0)),
            pl.BlockSpec((width, width), lambda w: (0, 0)),
        ],
        out_shape=[
            jax.ShapeDtypeStruct((3, 3, WIN, WIN, width), bf16),
            jax.ShapeDtypeStruct((width, width), f32),
        ],
        scratch_shapes=[pltpu.VMEM((4, WIN, WIN, width), bf16)],
        compiler_params=pltpu.CompilerParams(vmem_limit_bytes=VMEM),
        cost_estimate=pl.CostEstimate(flops=10**10, bytes_accessed=10**7, transcendentals=0),
        name="attend_early",
    )(*[a for a in arrays for _ in range(4)], codes, out_weight, bias, bias, bias)


def late_kernel(*refs):
    parts, refs = refs[:8], refs[8:]
    up_ref, down_ref, corner_ref, left_ref, code_ref, code_above_ref, w_ref, before_ref = refs[:8]
    bias_refs, half_ref, refs = refs[8:11], refs[11], refs[12:]
    own_ref, below_ref, above_ref, corner_out_ref, right_ref, keep_ref, give_ref, cells_ref, ws_ref = refs
    window = pl.program_id(0)

    @pl.when(window == 0)
    def _():
        ws_ref[...] = before_ref[...]

    @pl.when(window < 2)
    def _():
        for i in range(4):
            cells_ref[i, :HALF] = up_ref[i, 0]
            cells_ref[i, HALF:] = merged(parts[2 * i + 1][...], parts[2 * i][...])

    @pl.when(window == 2)
    def _():
        for i in range(4):
            cells_ref[i, :HALF] = merged(parts[2 * i + 1][...], parts[2 * i][...])
            cells_ref[i, HALF:] = down_ref[i, :HALF]

    @pl.when(window == 3)
    def _():
        for i in range(4):
            cells_ref[i, :HALF] = merged(unpack(left_ref[i])[:HALF], parts[2 * i][...])
            cells_ref[i, HALF:] = merged(unpack(corner_ref[i]), unpack(down_ref[i, HALF:]))

    @pl.when(window == 4)
    def _():
        for i in range(4):
            beside = unpack(left_ref[i])
            cells_ref[i, :HALF] = merged(beside[16:], parts[2 * i + 1][...])
            cells_ref[i, HALF:] = merged(beside[8:16], parts[2 * i][...])

    above = (window == 2) | (window == 3)
    code_row = jnp.where(above, code_above_ref[0], code_ref[0, 0])

    def store(lanes, *grads):
        for i, grad in enumerate(grads):
            own_ref[i, 0, :, :, lanes] = grad.reshape(WIN, WIN, LANES)

    ws_ref[...] += window_pass(
        lambda i, lanes: cells_ref[i, :, :, lanes].reshape(TOKENS, -1), code_row, w_ref, bias_refs, store
    )

    for w in range(2):

        @pl.when(window == w)
        def _():
            for i in range(3):
                below_ref[i, w] = own_ref[i, 0, :HALF]

    @pl.when(window == 2)
    def _():
        for i in range(3):
            above_ref[i, :HALF] = own_ref[i, 0, HALF:]

    @pl.when(window == 4)
    def _():
        for i in range(3):
            right_ref[i, 4:] = pack_low(own_ref[i, 0])
        rows = keep_ref.shape[0]
        keep_ref[...] = ws_ref[pl.ds(pl.multiple_of(half_ref[0] * rows, 8), rows)]
        give_ref[...] = ws_ref[pl.ds(pl.multiple_of((1 - half_ref[0]) * rows, 8), rows)]

    @pl.when(window == 3)
    def _():
        for i in range(3):
            above_ref[i, HALF:] = pack_high(own_ref[i, 0, HALF:])
            corner_out_ref[i] = pack_low(own_ref[i, 0, HALF:])
            right_ref[i, :4] = pack_low(own_ref[i, 0, :HALF])


def attend_late(arrays, borrowed, codes, codes_above, out_weight, bias, before, half):
    width = arrays[0].shape[-1]
    fixed = lambda shape: pl.BlockSpec(shape, lambda w, n=len(shape): (0,) * n)

    def rows_of(w, side):
        return jnp.where(w < 2, 3, jnp.where(w < 4, 0, 1 + side))

    parts = [
        pl.BlockSpec((HALF, WIN, width), lambda w: (rows_of(w, 0), jnp.minimum(w, 3), 0)),
        pl.BlockSpec((HALF, WIN, width), lambda w: (rows_of(w, 1), jnp.minimum(w + 1, 3), 0)),
    ]
    up_spec = pl.BlockSpec((4, 1, HALF, WIN, width), lambda w: (0, jnp.minimum(w, 1), 0, 0, 0))
    back = [(3, 2, HALF, WIN, width), (3, 12, WIN, width), (3, 4, WIN, width), (3, 12, WIN, width)]
    return pl.pallas_call(
        late_kernel,
        grid=(5,),
        in_specs=parts * 4
        + [up_spec]
        + [fixed(b.shape) for b in borrowed[1:]]
        + [
            pl.BlockSpec(
                (1, 1, 1, TOKENS),
                lambda w: (jnp.where(w < 4, 1, 0), jnp.where(w < 2, w, 3), 0, 0),
            ),
            pl.BlockSpec((1, 1, TOKENS), lambda w: (jnp.where(w == 3, 1, 0), 0, 0)),
            fixed((width, width)),
            fixed((width, width)),
        ]
        + bias_specs()
        + [pl.BlockSpec(memory_space=pltpu.SMEM)],
        out_specs=[pl.BlockSpec((3, 1, WIN, WIN, width), lambda w: (0, w, 0, 0, 0))]
        + [fixed(s) for s in back]
        + [fixed((width // 2, width))] * 2,
        out_shape=[jax.ShapeDtypeStruct((3, 5, WIN, WIN, width), bf16)]
        + [jax.ShapeDtypeStruct(s, bf16) for s in back]
        + [jax.ShapeDtypeStruct((width // 2, width), f32)] * 2,
        scratch_shapes=[
            pltpu.VMEM((4, WIN, WIN, width), bf16),
            pltpu.VMEM((width, width), f32),
        ],
        compiler_params=pltpu.CompilerParams(vmem_limit_bytes=VMEM),
        cost_estimate=pl.CostEstimate(flops=2 * 10**10, bytes_accessed=2 * 10**7, transcendentals=0),
        name="attend_late",
    )(
        *[a for a in arrays for _ in range(2)],
        *borrowed,
        codes,
        codes_above,
        out_weight,
        before,
        bias,
        bias,
        bias,
        half,
    )


def unpack_kernel(early_ref, late_ref, below_ref, above_ref, corner_ref, left_ref, out):
    left, edge = unpack(left_ref[0, 4:]), unpack(left_ref[0, :4])
    above = unpack(above_ref[0, HALF:])

    def put(half, tiles):
        for t in range(4):
            rows = slice(HALF * half, HALF * (half + 1))
            out[rows, WIN * t : WIN * (t + 1), :] = merged(tiles[t], tiles[t + 1])

    put(0, [edge, below_ref[0, 0], below_ref[0, 1], late_ref[0, 2, :HALF], late_ref[0, 3, :HALF]])
    for half, rows in ((1, slice(HALF, WIN)), (2, slice(0, HALF))):
        own = [early_ref[0, w, rows] for w in range(3)] + [late_ref[0, 4, rows]]
        put(half, [left[rows]] + own)
    put(
        3,
        [unpack(corner_ref[0]), late_ref[0, 0, HALF:], late_ref[0, 1, HALF:], above_ref[0, :HALF], above],
    )


def unpack_one(which, pieces, width):
    out = (32, 64, width)
    return pl.pallas_call(
        unpack_kernel,
        grid=(1,),
        in_specs=[
            pl.BlockSpec((1,) + p.shape[1:], lambda i, n=p.ndim: (which,) + (0,) * (n - 1))
            for p in pieces
        ],
        out_specs=pl.BlockSpec(out, lambda i: (0, 0, 0)),
        out_shape=jax.ShapeDtypeStruct(out, bf16),
        compiler_params=pltpu.CompilerParams(vmem_limit_bytes=VMEM),
        cost_estimate=pl.CostEstimate(flops=10**6, bytes_accessed=3 * 10**6, transcendentals=0),
        name="unpack",
    )(*pieces)


def shifted(axis, distance):
    n = lax.axis_size(axis)
    return [(i, (i + distance) % n) for i in range(n)]


def shifted_both(row_distance, col_distance):
    rows, cols = lax.axis_size("rows"), lax.axis_size("cols")
    return [
        (r * cols + c, (r + row_distance) % rows * cols + (c + col_distance) % cols)
        for r in range(rows)
        for c in range(cols)
    ]


def xor_partners(axis, mask):
    n = 8 if axis == ("cols", "views") else lax.axis_size(axis)
    return [(i, i ^ mask) for i in range(n)]


def sum_over_all(keep, give, between):
    place = lax.axis_index("cols") * 2 + lax.axis_index("views")
    near = ("cols", "views")
    masks = (2, 1, 5)
    labels = (place // 2 % 2, (place ^ place // 4) % 2, place // 4)
    share = between(0, keep + lax.ppermute(give, near, xor_partners(near, masks[0])))
    for step in (1, 2):
        half = share.shape[0] // 2
        keep = lax.dynamic_slice_in_dim(share, labels[step] * half, half)
        give = lax.dynamic_slice_in_dim(share, (1 - labels[step]) * half, half)
        share = between(step, keep + lax.ppermute(give, near, xor_partners(near, masks[step])))
    for step, mask in enumerate((8, 24, 1, 3, 7)):
        share = between(3 + step, share + lax.ppermute(share, "rows", xor_partners("rows", mask)))
    share = share.astype(bf16)
    for mask, bit in zip(masks[::-1], labels[::-1]):
        other = lax.ppermute(share, near, xor_partners(near, mask))
        share = jnp.where(bit == 0, jnp.concatenate([share, other]), jnp.concatenate([other, share]))
    return share.astype(f32)


def body(queries, key_rows, value_rows, grad_out, regions, flip_view, bias_table, out_weight):
    arrays = [array[0] for array in (queries, key_rows, value_rows, grad_out)]
    width = arrays[0].shape[-1]
    tile_h, tile_w = arrays[0].shape[:2]
    band_h = tile_h * lax.axis_size("rows")
    band_w = tile_w * lax.axis_size("cols")
    up, down, left = shifted("rows", -1), shifted("rows", 1), shifted("cols", -1)

    to_up, to_down, to_corner, to_left = pack(arrays)
    to_left, regions, flip_view = lax.optimization_barrier((to_left, regions, flip_view))
    borrowed = [
        lax.ppermute(to_up, "rows", up),
        lax.ppermute(to_down, "rows", down),
        lax.ppermute(to_corner, ("rows", "cols"), shifted_both(1, -1)),
        lax.ppermute(to_left, "cols", left),
    ]

    row_pos = (lax.axis_index("rows") * tile_h + jnp.arange(tile_h, dtype=jnp.int32) + HALF) % band_h
    col_pos = (lax.axis_index("cols") * tile_w + jnp.arange(tile_w, dtype=jnp.int32) + HALF) % band_w
    key_code = (
        regions[0] * 4
        + (row_pos < HALF).astype(jnp.int32)[:, None] * 2
        + (col_pos < HALF).astype(jnp.int32)[None, :]
    )
    codes = key_code.reshape(2, WIN, 4, WIN).transpose(0, 2, 1, 3)
    codes = jnp.roll(codes, (HALF, HALF), axis=(2, 3)).reshape(2, 4, 1, TOKENS)
    codes_above = lax.ppermute(codes[1, 2:], "rows", down)

    bias = build_bias(bias_table, flip_view[0])

    early, early_sum = attend_early(arrays, codes, out_weight, bias)
    core = lax.axis_index("cols") % 2
    late, to_below, to_above, to_corner, to_right, keep, give = attend_late(
        arrays, borrowed, codes, codes_above, out_weight, bias, early_sum, core[None]
    )

    home = [
        lax.ppermute(to_below, "rows", down),
        lax.ppermute(to_above, "rows", up),
        lax.ppermute(to_corner, ("rows", "cols"), shifted_both(-1, 1)),
        lax.ppermute(to_right, "cols", shifted("cols", 1)),
    ]
    grads = []

    def between(step, share):
        if step >= 5:
            grads.append(unpack_one(step - 5, [early, late, *home], width))
            share, grads[-1] = lax.optimization_barrier((share, grads[-1]))
        if 4 <= step < 7:
            share, *home[:] = lax.optimization_barrier((share, *home))
        return share

    weight_total = sum_over_all(keep, give, between)
    factor = jnp.minimum(1.0, clip_norm / jnp.sqrt(jnp.sum(weight_total * weight_total) + 1e-06))
    grad_weight = weight_total * factor
    return (grads[0][None], grads[1][None], grads[2][None], grad_weight)


def solution(mesh):
    return jax.shard_map(
        body,
        mesh=mesh,
        in_specs=(
            P("views", "rows", "cols", None),
            P("views", "rows", "cols", None),
            P("views", "rows", "cols", None),
            P("views", "rows", "cols", None),
            P("views", "rows", "cols"),
            P("views"),
            P(),
            P(),
        ),
        out_specs=(
            P("views", "rows", "cols", None),
            P("views", "rows", "cols", None),
            P("views", "rows", "cols", None),
            P(),
        ),
        check_vma=False,
    )
```
